512 devices in a mesh: streams: 16 (over y, core), tp: 32 (over x, z).
Axes of the slice: x: 4, y: 8, z: 8, core: 2. Of those that a mesh axis runs over, the one named last changes fastest.
Arguments:
- hidden_in: bfloat16 [512, 4, 1024], P(('streams', 'tp')), may hold values from -6 to 6
- byte_qkv: bfloat16 [512, 4, 1536], P(('streams', 'tp'))
- byte_cache: bfloat16 [512, 256, 512], P(('streams', 'tp'))
- byte_len: int32 [512], P(('streams', 'tp')), may hold values from 2 to 256, as said below
- flags: int32 [512, 4], P(('streams', 'tp')), may hold values 0 or 1
- coarse_prev: bfloat16 [512, 1024], P(('streams', 'tp')), may hold values from -6 to 6
- owner_map: int32 [32, 16, 1], replicated, may hold values from 0 to 15; in each aligned block of 16 rows (0 to 15, 16 to 31, ..., all dimensions but the last counted through in order) at most 2 rows name the same one
- up_weight: bfloat16 [1024, 8192], P(None, 'tp'), may hold values from -0.1875 to 0.1875
- coarse_gain: float32 [8192], replicated, may hold values from 0.5 to 1.5
- query_weight: bfloat16 [8192, 4096], P(None, 'tp'), may hold values from -0.0625 to 0.0625
- keyval_weight: bfloat16 [8192, 1024], P('tp'), may hold values from -0.0625 to 0.0625
- return_weight: bfloat16 [4096, 1024], P('tp'), may hold values from -0.09375 to 0.09375
- coarse_cache: bfloat16 [16, 64, 32, 32, 256], P('streams', None, 'tp'), as said below
- coarse_len: int32 [16, 64], P('streams'), may hold values from 1 to 32, as said below
Outputs:
- byte_out: bfloat16 [512, 4, 1024], P(('streams', 'tp'))
The draws below stay inside these ranges and needn't reach their ends.
Inputs may be any that keep to these rules, and one draw needn't show every extreme that they name: `owner_map`: within one index c of tp, no group owns more than 2 of the sequences s * 32 + c, and some group owns exactly 2. `byte_len`: some sequence has exactly 256 filled positions. `coarse_len`: some slot has exactly 32 filled positions. `coarse_cache`: the copies for heads h and h2 are equal where h // 8 = h2 // 8.
All inputs are finite; a program needn't handle non-finite values. No bound on the sum of `flags` on one device may be relied on, other than what follows from the above.
Results may differ from the reference program's by a relative error of at most 0.014.
Values may be sent and summed in bfloat16 or wider, within the bound.
A program may use at most 64 MiB of HBM per device.

```python
import math
import jax
import jax.numpy as jnp
import numpy as np
from jax import lax

DB = 1024
HD = 128
BKV = 2
BH = 8
DC = 8192
KVH = 4
COLUMNS = 32
HEADS = 32
NG = 16
STREAMS = 512
OWNED_MOST = 2
SLOTS = 64
LB = 256
LC = 32
STEPS = 4


def byte_key_base(key):
    return jax.random.normal(key, (STREAMS, LB, 2 * BKV * HD), jnp.float32)


def draw_byte_cache(key, part):
    drawn_keys = byte_key_base(key)
    return drawn_keys.astype(jnp.bfloat16)


def draw_byte_qkv(key, part):
    key = jax.random.fold_in(key, 22)
    total_width = BH * HD + 2 * BKV * HD
    values_drawn = jax.random.normal(key, (STREAMS, STEPS, total_width), jnp.float32)
    return values_drawn.astype(jnp.bfloat16)


def draw_coarse_cache(key, part):
    key = jax.random.fold_in(key, 23)
    first_key = jax.random.fold_in(key, 0)
    drawn_keys = jax.random.normal(first_key, (NG, SLOTS, KVH, LC, 2 * HD), jnp.float32)
    return jnp.repeat(drawn_keys, HEADS // KVH, axis=2).astype(jnp.bfloat16)


def draw_byte_len(key, part):
    key = jax.random.fold_in(key, 24)
    lengths = jax.random.randint(key, (STREAMS,), 2, LB + 1, jnp.int32)
    return jnp.where(jnp.arange(STREAMS) == 0, LB, lengths).astype(jnp.int32)


def draw_coarse_len(key, part):
    key = jax.random.fold_in(key, 25)
    lengths = jax.random.randint(key, (NG, SLOTS), 1, LC + 1, jnp.int32)
    first_slot = (jnp.arange(NG)[:, None] == 0) & (jnp.arange(SLOTS)[None, :] == 0)
    return jnp.where(first_slot, LC, lengths).astype(jnp.int32)


def plant(entries, rng, smallest, high):
    longest = entries.shape.index(max(entries.shape))
    spots = []
    for shift in (0, 1):
        where = [jax.random.randint(jax.random.fold_in(rng, axis), (), 0, length) for axis, length in enumerate(entries.shape)]
        where[longest] = (where[longest] + shift) % entries.shape[longest]
        spots.append(tuple(where))
    return entries.at[spots[0]].set(smallest).at[spots[1]].set(high)


def steps_of(own_key, dims, shards, low, top_value):
    level, own = 1.0, jax.random.fold_in(own_key, 6)
    for dim, blocks in shards:
        heights = jnp.exp(jax.random.uniform(jax.random.fold_in(own, dim), (blocks,), jnp.float32, low / len(shards), top_value / len(shards)))
        level = level * jnp.repeat(heights, dims[dim] // blocks).reshape([-1 if axis == dim else 1 for axis in range(len(dims))])
    return level


def assign_block(key, own, number, rows, number_of, top, limit, slope):
    order = jax.random.permutation(key, number_of)
    packed, usual = load_shares(number_of, rows * top, limit, slope, True), load_shares(number_of, rows * top, limit, slope, False)
    places = jnp.arange(number_of)

    def named(sizes, offset_by):
        used = int((sizes > 0).sum())
        fixed = max(1, used // 4)
        moved = fixed + (places - fixed + offset_by * (used - fixed)) % max(1, number_of - fixed)
        return jnp.zeros((number_of,), jnp.int32).at[order[jnp.where(places < fixed, places, moved)]].set(jnp.asarray(sizes, jnp.int32))

    sizes = jnp.where(number % 4 == 0, named(packed, number // 4), named(usual, number - number // 4 - 1))
    mixed = jax.random.permutation(jax.random.fold_in(own, 3), number_of)
    donor, sink = mixed[0:number_of // 2 * 2:2], mixed[1:number_of // 2 * 2:2]
    margin = jnp.minimum(sizes[donor] - 1, limit - sizes[sink]) // 2
    margin = jnp.where((donor == order[0]) | (sink == order[0]) | (sizes[sink] == 0), 0, jnp.maximum(margin, 0))
    moved = jax.random.randint(jax.random.fold_in(own, 4), (number_of // 2,), 0, 1 << 20) % (margin + 1)
    sizes = sizes.at[donor].add(-moved).at[sink].add(moved)
    members = jnp.searchsorted(jnp.cumsum(sizes), jnp.arange(rows * top), side="right").astype(jnp.int32)
    table = members.reshape(top, rows).T
    table = table[jax.random.permutation(jax.random.fold_in(own, 1), rows)]
    offset_by = jax.random.randint(jax.random.fold_in(own, 2), (rows, 1), 0, top)
    return jnp.take_along_axis(table, (jnp.arange(top)[None, :] + offset_by) % top, axis=1)


def load_shares(amount, total, limit, slope, full):
    loads = [(1 << 20) // math.isqrt(rank ** slope) + 1 for rank in range(1, amount + 1)]
    largest = limit if full else min(limit, max(-(-total // amount), total * loads[0] // sum(loads)))
    least = 1 if total - largest >= amount - 1 else 0
    given, surplus = [largest] + [least] * (amount - 1), total - largest - least * (amount - 1)
    while surplus > 0:
        candidates = [i for i in range(1, amount) if given[i] < largest] or [i for i in range(1, amount) if given[i] < limit]
        pool, left = sum([loads[i] for i in candidates]), surplus
        for i in candidates:
            more = min(limit - given[i], max(1, left * loads[i] // pool), surplus)
            given[i] = given[i] + more
            surplus = surplus - more
    return np.array(given)


def centred(key, dims, spread, most, shards=(), held_as=jnp.bfloat16):
    level = steps_of(key, dims, shards, -0.22, 0.18) if shards else 1.0
    drawn = jax.random.normal(key, dims, jnp.float32) * spread * level
    return jnp.minimum(jnp.maximum(drawn, -most), most).astype(held_as)


def setup_inputs(seed: int = 0) -> dict:
    splits = jax.random.split(jax.random.key(seed), 15)
    hidden_in = centred(splits[0], (STREAMS, STEPS, DB), 1.0, 6.0, ((0, 512),))
    byte_qkv = draw_byte_qkv(jax.random.fold_in(splits[14], 71), 0)
    byte_cache = draw_byte_cache(jax.random.fold_in(splits[14], 71), 0)
    byte_len = draw_byte_len(jax.random.fold_in(splits[14], 71), 0)
    flags = plant((jax.random.randint(splits[4], (STREAMS, STEPS), 0, 2) < 1).astype(jnp.int32), jax.random.fold_in(splits[4], 1), 0, 1)
    coarse_prev = centred(splits[5], (STREAMS, DB), 1.0, 6.0, ((0, 512),))
    owner_map_keys = jax.random.split(jax.random.fold_in(splits[6], 1), COLUMNS * NG // NG)
    owner_map_turns = jax.random.permutation(jax.random.fold_in(splits[6], 3), COLUMNS * NG // NG)
    owner_map = jax.vmap(lambda own, number: assign_block(jax.random.fold_in(splits[6], 2), own, number, NG, NG, 1, OWNED_MOST, 2))(owner_map_keys, owner_map_turns).reshape((COLUMNS, NG, 1))
    up_weight = centred(splits[7], (DB, DC), DB ** -0.5, 0.1875, ((1, 32),))
    coarse_gain = jnp.clip(1.0 + 0.1 * jax.random.normal(splits[8], (DC,), jnp.float32), 0.5, 1.5)
    query_weight = centred(splits[9], (DC, HEADS * HD), DC ** -0.5, 0.0625, ((1, 32),))
    keyval_weight = centred(splits[10], (DC, 2 * KVH * HD), DC ** -0.5, 0.0625, ((0, 32),))
    return_weight = centred(splits[11], (HEADS * HD, DB), (HEADS * HD) ** -0.5, 0.09375, ((0, 32),))
    coarse_cache = draw_coarse_cache(jax.random.fold_in(splits[14], 71), 0)
    coarse_len = draw_coarse_len(jax.random.fold_in(splits[14], 71), 0)
    return dict(hidden_in=hidden_in, byte_qkv=byte_qkv, byte_cache=byte_cache, byte_len=byte_len, flags=flags, coarse_prev=coarse_prev, owner_map=owner_map, up_weight=up_weight, coarse_gain=coarse_gain, query_weight=query_weight, keyval_weight=keyval_weight, return_weight=return_weight, coarse_cache=coarse_cache, coarse_len=coarse_len)


EPSILON = 1e-05
NEG_FILL = -1e+30

def split_softmax(scores_old, scores_new):
    largest = jnp.maximum(lax.optimization_barrier(jnp.max(scores_old, axis=-1, keepdims=True)), lax.optimization_barrier(jnp.max(scores_new, axis=-1, keepdims=True)))
    exp_old = jnp.exp(scores_old - largest)
    exp_new = jnp.exp(scores_new - largest)
    denominator = lax.optimization_barrier(jnp.sum(exp_old, axis=-1, keepdims=True)) + lax.optimization_barrier(jnp.sum(exp_new, axis=-1, keepdims=True))
    return ((exp_old / denominator).astype(jnp.bfloat16), (exp_new / denominator).astype(jnp.bfloat16))

def rank_table(owner_map):
    owners = owner_map[:, :, 0]
    group_total = owners.shape[1]
    same_owner = owners[:, :, None] == owners[:, None, :]
    earlier = jnp.arange(group_total, dtype=jnp.int32)[None, :, None] > jnp.arange(group_total, dtype=jnp.int32)[None, None, :]
    ranking = lax.optimization_barrier(jnp.sum((same_owner & earlier).astype(jnp.int32), axis=2))
    return (owners, ranking)

def byte_attention(byte_qkv, byte_cache, byte_len):
    number, step_count, total_width = byte_qkv.shape
    length = byte_cache.shape[1]
    kv_width = byte_cache.shape[2] // 2
    kv_groups = kv_width // HD
    head_count = (total_width - 2 * kv_width) // HD
    group_size = head_count // kv_groups
    query_part = byte_qkv[:, :, :head_count * HD].astype(jnp.float32).reshape(number, step_count, kv_groups, group_size, HD)
    new_keys = byte_qkv[:, :, head_count * HD:head_count * HD + kv_width].astype(jnp.float32).reshape(number, step_count, kv_groups, HD)
    new_values = byte_qkv[:, :, head_count * HD + kv_width:].astype(jnp.float32).reshape(number, step_count, kv_groups, HD)
    old_keys = byte_cache[:, :, :kv_width].astype(jnp.float32).reshape(number, length, kv_groups, HD)
    old_values = byte_cache[:, :, kv_width:].astype(jnp.float32).reshape(number, length, kv_groups, HD)
    scaling = HD ** (-0.5)
    scores_old = jnp.einsum('nsgjd,nlgd->nsgjl', query_part, old_keys) * scaling
    valid_old = jnp.arange(length, dtype=jnp.int32)[None, :] < byte_len[:, None]
    scores_old = jnp.where(valid_old[:, None, None, None, :], scores_old, NEG_FILL)
    scores_new = jnp.einsum('nsgjd,nugd->nsgju', query_part, new_keys) * scaling
    causal = jnp.arange(step_count)[:, None] >= jnp.arange(step_count)[None, :]
    scores_new = jnp.where(causal[None, :, None, None, :], scores_new, NEG_FILL)
    weights_old, weights_new = split_softmax(scores_old, scores_new)
    mixed_heads = jnp.einsum('nsgjl,nlgd->nsgjd', weights_old.astype(jnp.float32), old_values)
    mixed_heads = mixed_heads + jnp.einsum('nsgju,nugd->nsgjd', weights_new.astype(jnp.float32), new_values)
    return mixed_heads.reshape(number, step_count, head_count * HD)

def reference(hidden_in, byte_qkv, byte_cache, byte_len, flags, coarse_prev, owner_map, up_weight, coarse_gain, query_weight, keyval_weight, return_weight, coarse_cache, coarse_len):
    number, step_count, byte_width = hidden_in.shape
    attended = byte_attention(byte_qkv, byte_cache, byte_len)
    byte_rows = (hidden_in.astype(jnp.float32) + attended).astype(jnp.bfloat16)
    owners, ranking = rank_table(owner_map)
    column_total = owners.shape[0]
    owner_of = owners.T.reshape(-1)
    slot_of = (jnp.arange(column_total, dtype=jnp.int32)[:, None] * OWNED_MOST + ranking).T.reshape(-1)
    flat_rows = byte_rows.reshape(number * step_count, byte_width)
    expanded = jnp.dot(flat_rows, up_weight, preferred_element_type=jnp.float32).astype(jnp.bfloat16)
    inverse = lax.rsqrt(lax.optimization_barrier(jnp.mean(jnp.square(expanded.astype(jnp.float32)), axis=1)) + EPSILON)[:, None]
    scaled = (expanded.astype(jnp.float32) * coarse_gain).astype(jnp.bfloat16)
    queries = (jnp.dot(scaled, query_weight, preferred_element_type=jnp.float32) * inverse).astype(jnp.bfloat16)
    head_count = query_weight.shape[1] // HD
    queries = queries.reshape(number, step_count, head_count, HD)
    keyvals = jnp.dot(scaled, keyval_weight, preferred_element_type=jnp.float32) * inverse
    kv_heads = keyval_weight.shape[1] // (2 * HD)
    new_keys = keyvals[:, :kv_heads * HD].astype(jnp.bfloat16).reshape(number, step_count, kv_heads, HD)
    new_values = keyvals[:, kv_heads * HD:].astype(jnp.bfloat16).reshape(number, step_count, kv_heads, HD)
    group_size = head_count // kv_heads
    cache_len = coarse_len[owner_of, slot_of]
    flag_on = flags > 0
    length = coarse_cache.shape[3]
    scaling = HD ** (-0.5)
    valid_old = jnp.arange(length, dtype=jnp.int32)[None, :] < cache_len[:, None]
    causal = jnp.arange(step_count)[:, None] >= jnp.arange(step_count)[None, :]
    valid_new = causal[None, :, :] & flag_on[:, None, :]

    def one_head(head):
        cache_head = lax.dynamic_index_in_dim(coarse_cache, head, 2, keepdims=False)[owner_of, slot_of].astype(jnp.float32)
        query_head = lax.dynamic_index_in_dim(queries, head, 2, keepdims=False).astype(jnp.float32)
        key_head = lax.dynamic_index_in_dim(new_keys, head // group_size, 2, keepdims=False).astype(jnp.float32)
        value_head = lax.dynamic_index_in_dim(new_values, head // group_size, 2, keepdims=False).astype(jnp.float32)
        scores_old = jnp.einsum('nsd,nld->nsl', query_head, cache_head[:, :, :HD]) * scaling
        scores_old = jnp.where(valid_old[:, None, :], scores_old, NEG_FILL)
        scores_new = jnp.einsum('nsd,nud->nsu', query_head, key_head) * scaling
        scores_new = jnp.where(valid_new, scores_new, NEG_FILL)
        weights_old, weights_new = split_softmax(scores_old, scores_new)
        mixed_head = jnp.einsum('nsl,nld->nsd', weights_old.astype(jnp.float32), cache_head[:, :, HD:])
        mixed_head = mixed_head + jnp.einsum('nsu,nud->nsd', weights_new.astype(jnp.float32), value_head)
        return mixed_head.astype(jnp.bfloat16)
    mixed_all = lax.map(one_head, jnp.arange(head_count, dtype=jnp.int32))
    mixed_all = jnp.transpose(mixed_all, (1, 2, 0, 3)).reshape(number * step_count, head_count * HD)
    returned = jnp.dot(mixed_all, return_weight, preferred_element_type=jnp.float32).astype(jnp.bfloat16)
    returned = returned.reshape(number, step_count, byte_width)
    current = coarse_prev.astype(jnp.float32)
    outputs = []
    for step in range(step_count):
        current = jnp.where(flags[:, step, None] > 0, returned[:, step].astype(jnp.float32), current)
        outputs.append(byte_rows[:, step].astype(jnp.float32) + current)
    return jnp.stack(outputs, axis=1).astype(jnp.bfloat16)
```

```python
import functools

import jax
import jax.numpy as jnp
from jax import lax
from jax.experimental import pallas as pl
from jax.experimental.pallas import tpu as pltpu
from jax.sharding import PartitionSpec as P

HD = 128
EPSILON = 1e-05
NEG_FILL = -1e30
F32, BF16, I32 = jnp.float32, jnp.bfloat16, jnp.int32
MESH = pl.DeviceIdType.MESH


def iota(shape, dim):
    return lax.broadcasted_iota(I32, shape, dim)


def dot(a, b):
    return lax.dot_general(a, b, (((1,), (0,)), ((), ())), preferred_element_type=F32)


def dot_t(a, b):
    return lax.dot_general(a, b, (((1,), (1,)), ((), ())), preferred_element_type=F32)


def bdot(a, b):
    return lax.dot_general(a, b, (((2,), (1,)), ((0,), (0,))), preferred_element_type=F32)


def bdot_t(a, b):
    return lax.dot_general(a, b, (((2,), (2,)), ((0,), (0,))), preferred_element_type=F32)


def kernel(
    S, X, Z,
    byte_len, flags, hidden, qkv, prev, owner_row, gain, coarse_len,
    byte_cache, up_hbm, query_hbm, keyval_hbm, return_hbm, cache_hbm,
    out_ref,
    bc, up, wq, wkv, wr, cc,
    qs, kn, os, xm,
    XS, XT, UT, MS, KP, KX, KZ, SQZ, SQX, PX, RX, PZ, RZ, RB,
    local_sem,
    xs_s, xs_r, ms_s, ms_r, rb_s, rb_r,
    xtz_s, xtz_r, xtx_s, xtx_r,
    utz_s, utz_r, utx_s, utx_r,
    kx_s, kx_r, kz_s, kz_r, sqz_s, sqz_r, sqx_s, sqx_r,
    px_s, px_r, pz_s, pz_r,
):
    T = X * Z
    me_s, me_t = lax.axis_index("streams"), lax.axis_index("tp")
    x, z = me_t // Z, me_t % Z
    rows_own = up.shape[0] // S

    locals_ = [
        pltpu.make_async_copy(up_hbm, up, local_sem.at[0]),
        pltpu.make_async_copy(byte_cache.at[0], bc, local_sem.at[1]),
        pltpu.make_async_copy(keyval_hbm, wkv, local_sem.at[2]),
        pltpu.make_async_copy(query_hbm, wq, local_sem.at[3]),
        pltpu.make_async_copy(cache_hbm.at[0, :, 0], cc, local_sem.at[4]),
        pltpu.make_async_copy(return_hbm, wr, local_sem.at[5]),
    ]
    for copy in locals_:
        copy.start()

    def s_peer(d):
        return (lax.rem(me_s + d, S), me_t)

    def z_peer(d):
        return (me_s, x * Z + lax.rem(z + d, Z))

    def x_peer(d):
        return (me_s, lax.rem(x + d, X) * Z + z)

    def loop(count, body):
        def step(d, carry):
            body(d)
            return carry

        lax.fori_loop(1, count, step, 0)

    def remote(src, dst, send, recv, peer):
        return pltpu.make_async_remote_copy(
            src_ref=src, dst_ref=dst, send_sem=send, recv_sem=recv,
            device_id=peer, device_id_type=MESH,
        )

    barrier = pltpu.get_barrier_semaphore()
    for count, peer in ((S, s_peer), (Z, z_peer), (X, x_peer)):
        loop(count, lambda d, peer=peer: pl.semaphore_signal(
            barrier, inc=1, device_id=peer(d), device_id_type=MESH))

    def spread(buf, me, count, peer, send, recv):
        loop(count, lambda d: remote(
            buf.at[me], buf.at[me], send.at[d], recv.at[d], peer(d)).start())

    def gathered(buf, me, count, peer, send, recv):
        def body(d):
            source = lax.rem(me + count - d, count)
            remote(buf.at[source], buf.at[source], send.at[d], recv.at[d], peer(d)).wait_recv()

        loop(count, body)

    def drained(buf, count, peer, send, recv):
        loop(count, lambda d: remote(
            buf.at[0], buf.at[0], send.at[d], recv.at[d], peer(d)).wait_send())

    def trade(src, dst, me, count, peer, send, recv):
        def body(d):
            other = lax.rem(me + d, count)
            remote(src.at[other], dst.at[me], send.at[d], recv.at[d], peer(d)).start()

        loop(count, body)

    def to_x(buf, zb, send, recv):
        loop(X, lambda d: remote(
            buf.at[x * Z + zb], buf.at[x * Z + zb],
            send.at[d, zb], recv.at[d, zb], x_peer(d)).start())

    def tp_start(buf, zs, zr, xs, xr):
        to_x(buf, z, xs, xr)
        loop(Z, lambda d: remote(
            buf.at[me_t], buf.at[me_t], zs.at[d], zr.at[d], z_peer(d)).start())

    def tp_forward(buf, zs, zr, xs, xr):
        def body(d):
            zb = lax.rem(z + Z - d, Z)
            block = buf.at[x * Z + zb]
            remote(block, block, zs.at[d], zr.at[d], z_peer(d)).wait_recv()
            to_x(buf, zb, xs, xr)

        loop(Z, body)

    def tp_arrived(buf, d, xs, xr):
        source = lax.rem(x + X - d, X)

        def body(zb, carry):
            block = buf.at[source * Z + zb]
            remote(block, block, xs.at[d, zb], xr.at[d, zb], x_peer(d)).wait_recv()
            return carry

        lax.fori_loop(0, Z, body, 0)

    def tp_drained(buf, zs, zr, xs, xr):
        drained(buf, Z, z_peer, zs, zr)

        def body(zb, carry):
            loop(X, lambda d: remote(
                buf.at[0], buf.at[0], xs.at[d, zb], xr.at[d, zb], x_peer(d)).wait_send())
            return carry

        lax.fori_loop(0, Z, body, 0)

    locals_[0].wait()
    own = up[pl.ds(pl.multiple_of(me_s * rows_own, rows_own), rows_own), :]
    UT[me_t] = (own.astype(F32) * gain[...]).astype(BF16)
    pl.semaphore_wait(barrier, S + Z + X - 3)
    tp_start(UT, utz_s, utz_r, utx_s, utx_r)

    locals_[2].wait()
    kv_heads = wkv.shape[1] // (2 * HD)
    partial = dot(UT[me_t], wkv[...]).astype(BF16)
    for j in range(kv_heads):
        KP[j] = jnp.concatenate(
            [partial[:, j * HD:(j + 1) * HD], partial[:, (kv_heads + j) * HD:(kv_heads + j + 1) * HD]],
            axis=1,
        )
    trade(KP, KX, x, X, x_peer, kx_s, kx_r)

    locals_[1].wait()
    steps = hidden.shape[1]
    kn[...] = jnp.zeros_like(kn)
    for i in range(2):
        for hh in range(4):
            qs[pl.ds(i * 16 + hh * 4, 4), :] = qkv[0, :, pl.ds((i * 4 + hh) * HD, HD)].astype(F32)
        kn[i, 0:4, :] = qkv[0, :, pl.ds((8 + i) * HD, HD)].astype(F32)
        kn[2 + i, 0:4, :] = qkv[0, :, pl.ds((10 + i) * HD, HD)].astype(F32)
    length = bc.shape[0]
    scaling = HD ** (-0.5)
    seen = iota((16, length), 1) < byte_len[0]
    causal = iota((16, 16), 1) <= iota((16, 16), 0) % 4
    for i in range(2):
        q_i = qs[pl.ds(i * 16, 16), :].astype(BF16)
        old = dot_t(q_i, bc[:, pl.ds(i * HD, HD)]) * scaling
        old = jnp.where(seen, old, NEG_FILL)
        new = dot_t(q_i, kn[i].astype(BF16)) * scaling
        new = jnp.where(causal, new, NEG_FILL)
        top = jnp.maximum(jnp.max(old, axis=1, keepdims=True), jnp.max(new, axis=1, keepdims=True))
        old, new = jnp.exp(old - top), jnp.exp(new - top)
        total = jnp.sum(old, axis=1, keepdims=True) + jnp.sum(new, axis=1, keepdims=True)
        old, new = (old / total).astype(BF16), (new / total).astype(BF16)
        os[pl.ds(i * 16, 16), :] = dot(old, bc[:, pl.ds((2 + i) * HD, HD)]) + dot(
            new, kn[2 + i].astype(BF16))
        for hh in range(4):
            xm[pl.ds((2 * i + hh // 2) * 4, 4), pl.ds((hh % 2) * HD, HD)] = (
                hidden[0, :, pl.ds((i * 4 + hh) * HD, HD)].astype(F32) + os[pl.ds(i * 16 + hh * 4, 4), :]
            )
    rows_16 = xm[...].astype(BF16)
    lanes = iota((16, HD), 1)
    marks = jnp.zeros((16, HD), F32)
    last = jnp.int32(-1)
    step_of_row = iota((16, 1), 0) % 4
    last_col = jnp.full((16, 1), -1, I32)
    for u in range(steps):
        mark = flags[0, u]
        marks = marks + jnp.where(lanes % 4 == u, mark.astype(F32), 0.0)
        last = jnp.where(mark > 0, jnp.int32(u), last)
        last_col = jnp.where(step_of_row == u, last, last_col)
    XS[me_s] = jnp.concatenate([rows_16, marks.astype(BF16)], axis=1)
    spread(XS, me_s, S, s_peer, xs_s, xs_r)

    tp_forward(UT, utz_s, utz_r, utx_s, utx_r)

    o_row = owner_row[...]
    eye = iota((S, S), 0) == iota((S, S), 1)
    o_col = jnp.sum(jnp.where(eye, o_row, 0.0), axis=1, keepdims=True)
    same = o_col == o_row
    rank_col = jnp.sum(
        jnp.where(same & (iota((S, S), 1) < iota((S, S), 0)), 1.0, 0.0), axis=1, keepdims=True)
    own_col = iota((S, 1), 0) == me_s
    my_owner = jnp.sum(jnp.where(own_col, o_col, 0.0), axis=0, keepdims=True)
    my_rank = jnp.sum(jnp.where(own_col, rank_col, 0.0), axis=0, keepdims=True)
    tgt_col = jnp.where(o_col == me_s.astype(F32), rank_col, -1.0)
    W = S * 16
    tgt = jnp.sum(
        jnp.where(iota((S, W), 1) // 16 == iota((S, W), 0), tgt_col, 0.0), axis=0, keepdims=True)

    gathered(XS, me_s, S, s_peer, xs_s, xs_r)
    r, l = iota((16, W), 0), iota((16, W), 1)
    every = XS[...].reshape(W, 256 + HD)
    picked = (tgt == ((r % 8) // 4).astype(F32)) & (l % 4 == r % 4)
    halves = []
    for part in range(2):
        pick = jnp.where(picked & ((l % 16) // 4 == (r // 8) * 2 + part), 1.0, 0.0).astype(BF16)
        halves.append(dot(pick, every[:, :256]).astype(BF16))
    slot_marks = []
    for j in range(2):
        pick = jnp.where((tgt == float(j)) & (l % 16 == 0), 1.0, 0.0).astype(BF16)
        slot_marks.append(dot(pick, every[:, 256:]))
    slot_marks = jnp.where((lanes % 8) // 4 == 0, slot_marks[0], slot_marks[1]).astype(BF16)
    XT[me_t] = jnp.concatenate(halves + [slot_marks], axis=1)
    tp_start(XT, xtz_s, xtz_r, xtx_s, xtx_r)

    def wait_trade(src, dst, me, count, peer, send, recv):
        def body(d):
            source = lax.rem(me + count - d, count)
            remote(src.at[0], dst.at[source], send.at[d], recv.at[d], peer(d)).wait_recv()

        loop(count, body)

    def total_of(own_part, buf, me, count):
        total = own_part.astype(F32)
        for d in range(1, count):
            total = total + buf[lax.rem(me + count - d, count)].astype(F32)
        return total

    wait_trade(KP, KX, x, X, x_peer, kx_s, kx_r)
    KZ[z] = total_of(KP[x], KX, x, X).astype(BF16)
    spread(KZ, z, Z, z_peer, kz_s, kz_r)

    tp_forward(XT, xtz_s, xtz_r, xtx_s, xtx_r)

    locals_[3].wait()

    def query_part(source, total):
        base = pl.multiple_of(source * (Z * 256), Z * 256)
        for zb in range(Z):
            total = total + dot(UT[source * Z + zb], wq[pl.ds(base + zb * 256, 256), :])
        return total

    folded = query_part(x, jnp.zeros((rows_own, HD), F32))
    for d in range(1, X):
        tp_arrived(UT, d, utx_s, utx_r)
        folded = query_part(lax.rem(x + X - d, X), folded)
    gathered(KZ, z, Z, z_peer, kz_s, kz_r)
    folded_kv = total_of(KZ[z], KZ, z, Z)
    MS[me_s] = jnp.concatenate([folded.astype(BF16), folded_kv.astype(BF16)], axis=1)
    spread(MS, me_s, S, s_peer, ms_s, ms_r)

    for d in range(1, X):
        tp_arrived(XT, d, xtx_s, xtx_r)
    rows_all = XT[:, :, :512].reshape(T * 16, 512)
    N = T * 8

    def project(top, bottom, width):
        upper = dot(rows_all, top).reshape(T, 16, width)[:, :8]
        lower = dot(rows_all, bottom).reshape(T, 16, width)[:, 8:]
        return (upper + lower).reshape(N, width)

    expanded = project(up[0:512, :], up[512:1024, :], up.shape[1]).astype(BF16).astype(F32)
    squared = expanded * expanded
    high = squared.astype(BF16)
    low = (squared - high.astype(F32)).astype(BF16)
    ones = jnp.ones((8, up.shape[1]), BF16)
    SQZ[z] = dot_t(ones, high) + dot_t(ones, low)
    spread(SQZ, z, Z, z_peer, sqz_s, sqz_r)
    gathered(SQZ, z, Z, z_peer, sqz_s, sqz_r)
    SQX[x] = total_of(SQZ[z], SQZ, z, Z)
    spread(SQX, x, X, x_peer, sqx_s, sqx_r)
    gathered(SQX, x, X, x_peer, sqx_s, sqx_r)
    squares = total_of(SQX[x], SQX, x, X)[0:1, :]
    inverse_row = lax.rsqrt(squares / (up.shape[1] * T) + EPSILON)
    inverse = jnp.sum(
        jnp.where(iota((N, N), 0) == iota((N, N), 1), inverse_row, 0.0), axis=1, keepdims=True)

    gathered(MS, me_s, S, s_peer, ms_s, ms_r)
    weights = MS[...].reshape(S * rows_own, 3 * HD)
    mixed = (project(weights[:512], weights[512:], 3 * HD) * inverse).astype(BF16)
    chunks = N // 32
    queries = mixed[:, :HD].reshape(chunks, 32, HD)
    keys = mixed[:, HD:2 * HD].reshape(chunks, 32, HD)
    values = mixed[:, 2 * HD:].reshape(chunks, 32, HD)

    locals_[4].wait()
    slots, span = cc.shape[0], cc.shape[1]
    cached = cc[...].reshape(chunks, 8 * span, 2 * HD)
    len_col = jnp.sum(
        jnp.where(iota((N, slots), 0) // 4 == iota((N, slots), 1), coarse_len[...].astype(F32), 0.0),
        axis=1, keepdims=True).reshape(chunks, 32, 1)
    wide = (32, 8 * span)
    position = jnp.where(
        iota(wide, 1) // span == iota(wide, 0) // 4, iota(wide, 1) % span, span).astype(F32)
    old = bdot_t(queries, cached[:, :, :HD]) * scaling
    old = jnp.where(position[None] < len_col, old, NEG_FILL)
    new = bdot_t(queries, keys) * scaling
    new_lane, new_row = iota((32, 32), 1), iota((32, 32), 0)
    allowed = (new_lane // 4 == new_row // 4) & (new_lane % 4 <= new_row % 4)
    mark_rows = []
    first_row = XT[:, 0:8, 512:].astype(F32).reshape(chunks, 4, 8, HD)
    for c in range(4):
        mark_rows.append(jnp.where(iota((1, 1, HD), 2) // 8 == c, first_row[:, c, 0:1, :], 0.0))
    mark_rows = (mark_rows[0] + mark_rows[1] + mark_rows[2] + mark_rows[3])[:, :, :32]
    new = jnp.where(allowed[None] & (mark_rows > 0.5), new, NEG_FILL)
    top = jnp.maximum(jnp.max(old, axis=2, keepdims=True), jnp.max(new, axis=2, keepdims=True))
    old, new = jnp.exp(old - top), jnp.exp(new - top)
    total = jnp.sum(old, axis=2, keepdims=True) + jnp.sum(new, axis=2, keepdims=True)
    old, new = (old / total).astype(BF16), (new / total).astype(BF16)
    attended = bdot(old, cached[:, :, HD:]) + bdot(new, values)
    attended = attended.astype(BF16).reshape(N, HD)

    locals_[5].wait()
    width = wr.shape[1]
    PX[...] = dot(attended, wr[...]).astype(BF16).reshape(X, Z * 8, width)
    trade(PX, RX, x, X, x_peer, px_s, px_r)
    wait_trade(PX, RX, x, X, x_peer, px_s, px_r)
    summed = total_of(PX[x], RX, x, X).reshape(Z, 8, width)
    PZ[...] = jnp.concatenate([summed[:, :, :512], summed[:, :, 512:]], axis=1).astype(BF16)
    trade(PZ, RZ, z, Z, z_peer, pz_s, pz_r)
    wait_trade(PZ, RZ, z, Z, z_peer, pz_s, pz_r)
    RB[me_s] = total_of(PZ[z], RZ, z, Z).astype(BF16)
    spread(RB, me_s, S, s_peer, rb_s, rb_r)
    gathered(RB, me_s, S, s_peer, rb_s, rb_r)

    back = RB[...].reshape(W, 512)
    lf = l.astype(F32)
    home = ((l // 16).astype(F32) == my_owner) & (((l % 8) // 4).astype(F32) == my_rank)
    home = home & (l % 4 == last_col) & ((l % 16) // 8 == r // 8)
    latest = jnp.zeros((16, 256), F32)
    for part in range(2):
        pick = jnp.where(home & ((r // 4) % 2 == part), 1.0, 0.0).astype(BF16)
        latest = latest + dot(pick, back[:, part * 256:(part + 1) * 256])
    earlier = jnp.zeros((16, 256), F32)
    for k in range(4):
        earlier = jnp.where(
            iota((16, 256), 0) // 4 == k, prev[0:1, pl.ds(k * 256, 256)].astype(F32), earlier)
    latest = jnp.where(last_col < 0, earlier, latest)
    xm[...] = rows_16.astype(F32) + latest
    for k in range(4):
        out_ref[0, :, pl.ds(k * 256, 256)] = xm[pl.ds(k * 4, 4), :].astype(BF16)

    for buf, count, peer, send, recv in (
        (XS, S, s_peer, xs_s, xs_r), (MS, S, s_peer, ms_s, ms_r), (RB, S, s_peer, rb_s, rb_r),
        (KX, X, x_peer, kx_s, kx_r), (KZ, Z, z_peer, kz_s, kz_r),
        (SQZ, Z, z_peer, sqz_s, sqz_r), (SQX, X, x_peer, sqx_s, sqx_r),
        (RX, X, x_peer, px_s, px_r), (RZ, Z, z_peer, pz_s, pz_r),
    ):
        drained(buf, count, peer, send, recv)
    tp_drained(UT, utz_s, utz_r, utx_s, utx_r)
    tp_drained(XT, xtz_s, xtz_r, xtx_s, xtx_r)


def shards(
    S, X, Z,
    hidden_in, byte_qkv, byte_cache, byte_len, flags, coarse_prev, owner_map, up_weight,
    coarse_gain, query_weight, keyval_weight, return_weight, coarse_cache, coarse_len,
):
    T = X * Z
    me_t = lax.axis_index("tp")
    part = up_weight.shape[1]
    gain = lax.dynamic_slice_in_dim(coarse_gain, me_t * part, part, 0)[None]
    owner_row = lax.dynamic_slice_in_dim(owner_map[:, :, 0], me_t, 1, 0).astype(F32)
    rows = up_weight.shape[0] // S
    heads2 = 2 * HD
    vm = pl.BlockSpec(memory_space=pltpu.VMEM)
    sm = pl.BlockSpec(memory_space=pltpu.SMEM)
    hbm = pl.BlockSpec(memory_space=pl.ANY)
    dma = pltpu.SemaphoreType.DMA
    pair = lambda *shape: [dma(shape), dma(shape)]
    scratch = [
        pltpu.VMEM(byte_cache.shape[1:], BF16),
        pltpu.VMEM(up_weight.shape, BF16),
        pltpu.VMEM(query_weight.shape, BF16),
        pltpu.VMEM(keyval_weight.shape, BF16),
        pltpu.VMEM(return_weight.shape, BF16),
        pltpu.VMEM((coarse_cache.shape[1],) + coarse_cache.shape[3:], BF16),
        pltpu.VMEM((32, HD), F32),
        pltpu.VMEM((4, 16, HD), F32),
        pltpu.VMEM((32, HD), F32),
        pltpu.VMEM((16, 256), F32),
        pltpu.VMEM((S, 16, 256 + HD), BF16),
        pltpu.VMEM((T, 16, 512 + HD), BF16),
        pltpu.VMEM((T, rows, part), BF16),
        pltpu.VMEM((S, rows, 3 * HD), BF16),
        pltpu.VMEM((X, rows, heads2), BF16),
        pltpu.VMEM((X, rows, heads2), BF16),
        pltpu.VMEM((Z, rows, heads2), BF16),
        pltpu.VMEM((Z, 8, T * 8), F32),
        pltpu.VMEM((X, 8, T * 8), F32),
        pltpu.VMEM((X, Z * 8, 1024), BF16),
        pltpu.VMEM((X, Z * 8, 1024), BF16),
        pltpu.VMEM((Z, 16, 512), BF16),
        pltpu.VMEM((Z, 16, 512), BF16),
        pltpu.VMEM((S, 16, 512), BF16),
        dma((6,)),
    ]
    for shape in (
        (S,), (S,), (S,), (Z,), (X, Z), (Z,), (X, Z), (X,), (Z,), (Z,), (X,), (X,), (Z,),
    ):
        scratch += pair(*shape)
    return pl.pallas_call(
        functools.partial(kernel, S, X, Z),
        out_shape=jax.ShapeDtypeStruct(hidden_in.shape, BF16),
        in_specs=[sm, sm] + [vm] * 6 + [hbm] * 6,
        out_specs=vm,
        scratch_shapes=scratch,
        compiler_params=pltpu.CompilerParams(
            collective_id=0, has_side_effects=True, vmem_limit_bytes=40 * 1024 * 1024
        ),
        name="decode",
    )(
        byte_len, flags, hidden_in, byte_qkv, coarse_prev, owner_row, gain, coarse_len,
        byte_cache, up_weight, query_weight, keyval_weight, return_weight, coarse_cache,
    )


def solution(mesh):
    S, T = mesh.shape["streams"], mesh.shape["tp"]
    X = 4 if T >= 16 else 2
    return jax.shard_map(
        functools.partial(shards, S, X, T // X),
        mesh=mesh,
        in_specs=(
            P(("streams", "tp"), None, None),
            P(("streams", "tp"), None, None),
            P(("streams", "tp"), None, None),
            P(("streams", "tp")),
            P(("streams", "tp"), None),
            P(("streams", "tp"), None),
            P(),
            P(None, "tp"),
            P(),
            P(None, "tp"),
            P("tp", None),
            P("tp", None),
            P("streams", None, "tp", None, None),
            P("streams", None),
        ),
        out_specs=P(("streams", "tp"), None, None),
        check_vma=False,
    )
```

```python
import functools

import jax
import jax.numpy as jnp
from jax import lax
from jax.experimental import pallas as pl
from jax.experimental.pallas import tpu as pltpu
from jax.sharding import PartitionSpec as P

HD = 128
EPSILON = 1e-05
NEG_FILL = -1e30
F32, BF16, I32 = jnp.float32, jnp.bfloat16, jnp.int32
MESH = pl.DeviceIdType.MESH


def iota(shape, dim):
    return lax.broadcasted_iota(I32, shape, dim)


def dot(a, b):
    return lax.dot_general(a, b, (((1,), (0,)), ((), ())), preferred_element_type=F32)


def dot_t(a, b):
    return lax.dot_general(a, b, (((1,), (1,)), ((), ())), preferred_element_type=F32)


def bdot(a, b):
    return lax.dot_general(a, b, (((2,), (1,)), ((0,), (0,))), preferred_element_type=F32)


def bdot_t(a, b):
    return lax.dot_general(a, b, (((2,), (2,)), ((0,), (0,))), preferred_element_type=F32)


def kernel(
    S, X, Z,
    byte_len_hbm, flags_hbm, hidden_hbm, qkv_hbm, prev_hbm, owner_hbm, gain_hbm, len_hbm,
    byte_cache, up_hbm, query_hbm, keyval_hbm, return_hbm, cache_hbm,
    out_ref,
    byte_len, flags, hidden, qkv, prev, owners, gain, coarse_len,
    first, bc, up, wq, wkv, wr, ck, cv,
    qs, kn, os, xm, raw, cols,
    XS, XT, UT, MQ, MK, KP, KX, KS, KZ, KA, SQZ, SQX, PX, RX, PZ, RZ, RB,
    local_sem,
    xs_sems, xt_sems, ut_sems, mq_sems, mk_sems, rb_sems,
    kx_s, kx_r, kz_s, kz_r, ka_s, ka_r, sqz_s, sqz_r, sqx_s, sqx_r,
    px_s, px_r, pz_s, pz_r,
):
    T = X * Z
    me_s, me_t = lax.axis_index("streams"), lax.axis_index("tp")
    x, z = me_t // Z, me_t % Z
    Y = S // 2
    y, core = me_s // 2, me_s % 2
    me_p = core * Y + y
    rows_own = first.shape[0]

    small = [
        pltpu.make_async_copy(gain_hbm.at[me_t], gain, local_sem.at[6]),
        pltpu.make_async_copy(hidden_hbm, hidden, local_sem.at[7]),
        pltpu.make_async_copy(qkv_hbm, qkv, local_sem.at[8]),
        pltpu.make_async_copy(prev_hbm, prev, local_sem.at[9]),
        pltpu.make_async_copy(owner_hbm.at[:, 0, :], owners, local_sem.at[10]),
        pltpu.make_async_copy(len_hbm, coarse_len, local_sem.at[11]),
        pltpu.make_async_copy(byte_len_hbm, byte_len, local_sem.at[12]),
        pltpu.make_async_copy(flags_hbm, flags, local_sem.at[13]),
    ]
    locals_ = [
        pltpu.make_async_copy(up_hbm, up, local_sem.at[0]),
        pltpu.make_async_copy(byte_cache.at[0], bc, local_sem.at[1]),
        pltpu.make_async_copy(keyval_hbm, wkv, local_sem.at[2]),
        pltpu.make_async_copy(query_hbm, wq, local_sem.at[3]),
        pltpu.make_async_copy(cache_hbm.at[0, :, 0, :, pl.ds(0, HD)], ck, local_sem.at[4]),
        pltpu.make_async_copy(return_hbm, wr, local_sem.at[5]),
        pltpu.make_async_copy(cache_hbm.at[0, :, 0, :, pl.ds(HD, HD)], cv, local_sem.at[14]),
    ]
    own_up = pltpu.make_async_copy(
        up_hbm.at[pl.ds(pl.multiple_of(me_p * rows_own, rows_own), rows_own)], first, local_sem.at[15])
    own_up.start()
    for copy in small + [locals_[2], locals_[1]]:
        copy.start()

    def y_peer(d):
        return (lax.rem(y + d, Y) * 2 + core, me_t)

    def core_peer(d):
        return (y * 2 + lax.rem(core + d, 2), me_t)

    def z_peer(d):
        return (me_s, x * Z + lax.rem(z + d, Z))

    def x_peer(d):
        return (me_s, lax.rem(x + d, X) * Z + z)

    def loop(count, body):
        def step(d, carry):
            body(d)
            return carry

        lax.fori_loop(1, count, step, 0)

    def remote(src, dst, send, recv, peer):
        return pltpu.make_async_remote_copy(
            src_ref=src, dst_ref=dst, send_sem=send, recv_sem=recv,
            device_id=peer, device_id_type=MESH,
        )

    barrier = pltpu.get_barrier_semaphore()
    for count, peer in ((Y, y_peer), (2, core_peer), (Z, z_peer), (X, x_peer)):
        loop(count, lambda d, peer=peer: pl.semaphore_signal(
            barrier, inc=1, device_id=peer(d), device_id_type=MESH))

    comms = []

    class Axis:
        def __init__(self, src, dst, me, count, peer, send, recv):
            self.src, self.dst, self.me, self.count = src, dst, me, count
            self.peer, self.send, self.recv_sem = peer, send, recv
            self.received = False
            comms.append(self)

        def copy(self, d, src, dst):
            return remote(src, dst, self.send.at[d], self.recv_sem.at[d], self.peer(d))

        def start(self):
            def body(d):
                other = self.me if self.src is self.dst else lax.rem(self.me + d, self.count)
                self.copy(d, self.src.at[other], self.dst.at[self.me]).start()

            loop(self.count, body)
            return self

        def recv(self):
            def body(d):
                block = self.dst.at[lax.rem(self.me + self.count - d, self.count)]
                self.copy(d, block, block).wait_recv()

            loop(self.count, body)
            self.received = True

        def total(self, own_part):
            if not self.received:
                self.recv()
            total = own_part.astype(F32)
            for d in range(1, self.count):
                total = total + self.dst[lax.rem(self.me + self.count - d, self.count)].astype(F32)
            return total

        def finish(self):
            if not self.received:
                self.recv()
            loop(self.count, lambda d: self.copy(d, self.dst.at[0], self.dst.at[0]).wait_send())

    class Plane:
        def __init__(self, buf, first, second, sems, whole):
            self.buf, self.whole = buf, whole
            (self.me1, self.n1, self.peer1), (self.me2, self.n2, self.peer2) = first, second
            self.s1, self.r1, self.s2, self.r2 = sems
            self.forwarded, self.got = False, set()
            comms.append(self)

        def place(self, i, j):
            return j * self.n1 + i

        def line(self, d, j):
            group = self.buf.at[pl.ds(j * self.n1, self.n1)]
            return remote(group, group, self.s2.at[d, 0], self.r2.at[d, 0], self.peer2(d))

        def hop1(self, d, block):
            return remote(block, block, self.s1.at[d], self.r1.at[d], self.peer1(d))

        def hop2(self, d, i, block):
            return remote(block, block, self.s2.at[d, i], self.r2.at[d, i], self.peer2(d))

        def onward(self, i):
            block = self.buf.at[self.place(i, self.me2)]
            loop(self.n2, lambda d: self.hop2(d, i, block).start())

        def start(self):
            block = self.buf.at[self.place(self.me1, self.me2)]
            if not self.whole:
                self.onward(self.me1)
            loop(self.n1, lambda d: self.hop1(d, block).start())
            return self

        def forward(self):
            def body(d):
                i = lax.rem(self.me1 + self.n1 - d, self.n1)
                self.hop1(d, self.buf.at[self.place(i, self.me2)]).wait_recv()
                if not self.whole:
                    self.onward(i)

            loop(self.n1, body)
            if self.whole:
                loop(self.n2, lambda d: self.line(d, self.me2).start())
            self.forwarded = True

        def each(self, body):
            def step(i, carry):
                body(i)
                return carry

            lax.fori_loop(0, self.n1, step, 0)

        def arrived(self, d):
            source = lax.rem(self.me2 + self.n2 - d, self.n2)
            if self.whole:
                self.line(d, source).wait_recv()
            else:
                self.each(
                    lambda i: self.hop2(d, i, self.buf.at[self.place(i, source)]).wait_recv())
            self.got.add(d)

        def recv(self):
            if not self.forwarded:
                self.forward()
            for d in range(1, self.n2):
                if d not in self.got:
                    self.arrived(d)

        def finish(self):
            self.recv()
            block = self.buf.at[0]
            loop(self.n1, lambda d: self.hop1(d, block).wait_send())
            if self.whole:
                loop(self.n2, lambda d: self.line(d, 0).wait_send())
            else:
                self.each(lambda i: loop(self.n2, lambda d: self.hop2(d, i, block).wait_send()))

    def over_tp(buf, sems, whole):
        return Plane(buf, (z, Z, z_peer), (x, X, x_peer), sems, whole)

    def over_streams(buf, sems):
        return Plane(buf, (y, Y, y_peer), (core, 2, core_peer), sems, True)

    small[0].wait()
    own_up.wait()
    gain_row = jnp.concatenate([gain[0:1, :], gain[1:2, :]], axis=1)
    UT[me_t] = (first[...].astype(F32) * gain_row).astype(BF16)
    pl.semaphore_wait(barrier, Y + Z + X - 2)
    ups = over_tp(UT, ut_sems, False).start()
    for copy in (locals_[0], locals_[3], locals_[4], locals_[6], locals_[5]):
        copy.start()

    locals_[2].wait()
    kv_heads = wkv.shape[1] // (2 * HD)
    partial = dot(UT[me_t], wkv[...]).astype(BF16)
    for j in range(kv_heads):
        KP[j] = jnp.concatenate(
            [partial[:, j * HD:(j + 1) * HD], partial[:, (kv_heads + j) * HD:(kv_heads + j + 1) * HD]],
            axis=1,
        )
    kv_x = Axis(KP, KX, x, X, x_peer, kx_s, kx_r).start()

    for copy in small[1:]:
        copy.wait()
    steps = hidden.shape[1]
    lanes = iota((16, HD), 1)
    marks = jnp.zeros((16, HD), F32)
    last = jnp.int32(-1)
    step_of_row = iota((16, 1), 0) % 4
    last_col = jnp.full((16, 1), -1, I32)
    for u in range(steps):
        mark = flags[0, u]
        marks = marks + jnp.where(lanes % 4 == u, mark.astype(F32), 0.0)
        last = jnp.where(mark > 0, jnp.int32(u), last)
        last_col = jnp.where(step_of_row == u, last, last_col)

    locals_[1].wait()
    kn[...] = jnp.zeros_like(kn)
    for i in range(2):
        for hh in range(4):
            qs[pl.ds(i * 16 + hh * 4, 4), :] = qkv[0, :, pl.ds((i * 4 + hh) * HD, HD)].astype(F32)
        kn[i, 0:4, :] = qkv[0, :, pl.ds((8 + i) * HD, HD)].astype(F32)
        kn[2 + i, 0:4, :] = qkv[0, :, pl.ds((10 + i) * HD, HD)].astype(F32)
    length = bc.shape[0]
    scaling = HD ** (-0.5)
    seen = iota((16, length), 1) < byte_len[0, 0]
    causal = iota((16, 16), 1) <= iota((16, 16), 0) % 4
    for i in range(2):
        q_i = qs[pl.ds(i * 16, 16), :].astype(BF16)
        old = dot_t(q_i, bc[:, pl.ds(i * HD, HD)]) * scaling
        old = jnp.where(seen, old, NEG_FILL)
        new = dot_t(q_i, kn[i].astype(BF16)) * scaling
        new = jnp.where(causal, new, NEG_FILL)
        top = jnp.maximum(jnp.max(old, axis=1, keepdims=True), jnp.max(new, axis=1, keepdims=True))
        old, new = jnp.exp(old - top), jnp.exp(new - top)
        total = jnp.sum(old, axis=1, keepdims=True) + jnp.sum(new, axis=1, keepdims=True)
        old, new = (old / total).astype(BF16), (new / total).astype(BF16)
        os[pl.ds(i * 16, 16), :] = dot(old, bc[:, pl.ds((2 + i) * HD, HD)]) + dot(
            new, kn[2 + i].astype(BF16))
        for hh in range(4):
            xm[pl.ds((2 * i + hh // 2) * 4, 4), pl.ds((hh % 2) * HD, HD)] = (
                hidden[0, :, pl.ds((i * 4 + hh) * HD, HD)].astype(F32) + os[pl.ds(i * 16 + hh * 4, 4), :]
            )
    rows_16 = xm[...].astype(BF16)
    XS[me_p] = jnp.concatenate([rows_16, marks.astype(BF16)], axis=1)
    rows_s = over_streams(XS, xs_sems).start()

    ups.forward()
    rows_s.forward()

    tiles = kv_x.total(KP[x]).astype(BF16)
    tall = rows_own // 16
    for b in range(2 * tall):
        KS[b // (2 * tall // Z), b % (2 * tall // Z)] = tiles[
            (b // 2) * 16:(b // 2 + 1) * 16, (b % 2) * HD:(b % 2 + 1) * HD]
    kv_z = Axis(KS, KZ, z, Z, z_peer, kz_s, kz_r).start()

    o_col = jnp.sum(
        jnp.where(iota((S, T), 1) == me_t, owners[...].astype(F32), 0.0), axis=1, keepdims=True)
    eye = iota((S, S), 0) == iota((S, S), 1)
    o_row = jnp.sum(jnp.where(eye, o_col, 0.0), axis=0, keepdims=True)
    same = o_col == o_row
    rank_col = jnp.sum(
        jnp.where(same & (iota((S, S), 1) < iota((S, S), 0)), 1.0, 0.0), axis=1, keepdims=True)
    own_col = iota((S, 1), 0) == me_s
    my_owner = jnp.sum(jnp.where(own_col, o_col, 0.0), axis=0, keepdims=True)
    my_rank = jnp.sum(jnp.where(own_col, rank_col, 0.0), axis=0, keepdims=True)
    tgt_col = jnp.where(o_col == me_s.astype(F32), rank_col, -1.0)
    W = S * 16
    stream_of = lambda lane: (lane // 16 % Y) * 2 + lane // (16 * Y)
    tgt = jnp.sum(
        jnp.where(stream_of(iota((S, W), 1)) == iota((S, W), 0), tgt_col, 0.0), axis=0, keepdims=True)

    rows_s.recv()
    r, l = iota((16, W), 0), iota((16, W), 1)
    every = XS[...].reshape(W, 256 + HD)
    picked = (tgt == ((r % 8) // 4).astype(F32)) & (l % 4 == r % 4)
    halves = []
    for part in range(2):
        pick = jnp.where(picked & ((l % 16) // 4 == (r // 8) * 2 + part), 1.0, 0.0).astype(BF16)
        halves.append(dot(pick, every[:, :256]).astype(BF16))
    XT[me_t] = jnp.concatenate(halves, axis=1)
    rows_t = over_tp(XT, xt_sems, True).start()
    slot_marks = []
    for j in range(2):
        pick = jnp.where((tgt == float(j)) & (l % 16 == 0), 1.0, 0.0).astype(BF16)
        slot_marks.append(dot(pick, every[:, 256:]))
    slot_marks = jnp.where((lanes % 8) // 4 == 0, slot_marks[0], slot_marks[1])[0:8, :]

    locals_[3].wait()

    def query_part(source, total):
        base = pl.multiple_of(source * (Z * 256), Z * 256)
        for zb in range(Z):
            total = total + dot(UT[source * Z + zb], wq[pl.ds(base + zb * 256, 256), :])
        return total

    folded = query_part(x, jnp.zeros((rows_own, HD), F32))
    KA[z] = kv_z.total(KS[z]).astype(BF16)
    kv_all = Axis(KA, KA, z, Z, z_peer, ka_s, ka_r).start()
    rows_t.forward()
    for d in range(1, X):
        ups.arrived(d)
        folded = query_part(lax.rem(x + X - d, X), folded)
        if d == 1:
            kv_all.recv()
            for b in range(2 * tall):
                MK[me_p, pl.ds((b // 2) * 16, 16), pl.ds((b % 2) * HD, HD)] = KA[
                    b // (2 * tall // Z), b % (2 * tall // Z)]
            keyvals_s = over_streams(MK, mk_sems).start()
    MQ[me_p] = folded.astype(BF16)
    queries_s = over_streams(MQ, mq_sems).start()

    locals_[0].wait()
    rows_t.recv()
    rows_all = XT[...].reshape(T * 16, 512)
    N = T * 8

    def project(top, bottom, width):
        upper = dot(rows_all, top).reshape(T, 16, width)[:, :8]
        lower = dot(rows_all, bottom).reshape(T, 16, width)[:, 8:]
        return (upper + lower).reshape(N, width)

    expanded = project(up[0:512, :], up[512:1024, :], up.shape[1]).astype(BF16).astype(F32)
    squared = expanded * expanded
    high = squared.astype(BF16)
    low = (squared - high.astype(F32)).astype(BF16)
    ones = jnp.ones((8, up.shape[1]), BF16)
    spot = slot_marks[:, :N] if N <= HD else jnp.concatenate([slot_marks] * (N // HD), axis=1)
    spot = jnp.where(iota((8, N), 1) // 8 == me_t, spot, 0.0)
    SQZ[z] = jnp.where(iota((8, N), 0) == 0, dot_t(ones, high) + dot_t(ones, low), spot)
    squares_z = Axis(SQZ, SQZ, z, Z, z_peer, sqz_s, sqz_r).start()
    keyvals_s.forward()
    queries_s.forward()
    SQX[x] = squares_z.total(SQZ[z])
    squares_x = Axis(SQX, SQX, x, X, x_peer, sqx_s, sqx_r).start()

    keyvals_s.recv()
    weights = MK[...].reshape(S * rows_own, 2 * HD)
    keyvals = project(weights[:512], weights[512:], 2 * HD)
    keys = keyvals[:, :HD].astype(BF16)
    queries_s.recv()
    weights = MQ[...].reshape(S * rows_own, HD)
    raw[...] = project(weights[:512], weights[512:], HD)

    locals_[4].wait()
    locals_[6].wait()
    locals_[5].wait()
    slots, span = ck.shape[0], ck.shape[1]
    len_col = jnp.sum(
        jnp.where(iota((N, slots), 0) // 4 == iota((N, slots), 1), coarse_len[...].astype(F32), 0.0),
        axis=1, keepdims=True)
    summed = squares_x.total(SQX[x])
    inverse_row = lax.rsqrt(summed[0:1, :] / (up.shape[1] * T) + EPSILON)
    marked = summed[1:2, :] > 0.5
    inverse = jnp.sum(
        jnp.where(iota((N, N), 0) == iota((N, N), 1), inverse_row, 0.0), axis=1, keepdims=True)
    cols[...] = jnp.where(iota((N, HD), 1) == 0, inverse, len_col)
    values = (keyvals[:, HD:] * inverse).astype(BF16)

    block, per = Z * 8, min(8, Z * 2)
    chunks = Z * 2 // per
    by_chunk = lambda col: col.reshape(chunks, per * 4, 1)
    row_old, lane_old = iota((per * 4, per * span), 0), iota((per * 4, per * span), 1)
    position = jnp.where(lane_old // span == row_old // 4, lane_old % span, span).astype(F32)
    lane_new, row_new = iota((block, N), 1), iota((block, N), 0)
    back_x = Axis(PX, RX, x, X, x_peer, px_s, px_r)
    for d in list(range(1, X)) + [0]:
        to = lax.rem(x + d, X)
        at_row = pl.ds(pl.multiple_of(to * block, block), block)
        at_slot = pl.ds(to * (Z * 2), Z * 2)
        queries = raw[at_row, :].astype(BF16)
        factor, filled = cols[at_row, 0:1] * scaling, cols[at_row, 1:2]
        old = bdot_t(queries.reshape(chunks, per * 4, HD), ck[at_slot].reshape(chunks, per * span, HD))
        new = dot_t(queries, keys)
        row = row_new + to * block
        allowed = (lane_new // 4 == row // 4) & (lane_new % 4 <= row % 4) & marked
        old = jnp.where(position[None] < by_chunk(filled), old * by_chunk(factor), NEG_FILL)
        new = jnp.where(allowed, new * factor * inverse_row, NEG_FILL)
        top = jnp.maximum(
            jnp.max(old, axis=2, keepdims=True).reshape(block, 1), jnp.max(new, axis=1, keepdims=True))
        old, new = jnp.exp(old - by_chunk(top)), jnp.exp(new - top)
        total = jnp.sum(old, axis=2, keepdims=True).reshape(block, 1) + jnp.sum(
            new, axis=1, keepdims=True)
        old, new = (old / by_chunk(total)).astype(BF16), (new / total).astype(BF16)
        attended = bdot(old, cv[at_slot].reshape(chunks, per * span, HD)).reshape(block, HD)
        attended = (attended + dot(new, values)).astype(BF16)
        PX[to] = dot(attended, wr[...]).astype(BF16)
        if d:
            back_x.copy(d, PX.at[to], RX.at[x]).start()

    summed = back_x.total(PX[x]).reshape(Z, 8, 1024)
    PZ[...] = jnp.concatenate([summed[:, :, :512], summed[:, :, 512:]], axis=1).astype(BF16)
    back_z = Axis(PZ, RZ, z, Z, z_peer, pz_s, pz_r).start()
    RB[me_p] = back_z.total(PZ[z]).astype(BF16)
    back_s = over_streams(RB, rb_sems).start()
    back_s.recv()

    home = (stream_of(l).astype(F32) == my_owner) & (((l % 8) // 4).astype(F32) == my_rank)
    home = home & (l % 4 == last_col) & ((l % 16) // 8 == r // 8)
    back = RB[...].reshape(W, 512)
    latest = jnp.zeros((16, 256), F32)
    for part in range(2):
        pick = jnp.where(home & ((r // 4) % 2 == part), 1.0, 0.0).astype(BF16)
        latest = latest + dot(pick, back[:, part * 256:(part + 1) * 256])
    earlier = jnp.zeros((16, 256), F32)
    for k in range(4):
        earlier = jnp.where(
            iota((16, 256), 0) // 4 == k, prev[0:1, pl.ds(k * 256, 256)].astype(F32), earlier)
    latest = jnp.where(last_col < 0, earlier, latest)
    xm[...] = rows_16.astype(F32) + latest
    for k in range(4):
        out_ref[0, :, pl.ds(k * 256, 256)] = xm[pl.ds(k * 4, 4), :].astype(BF16)

    for comm in comms:
        comm.finish()


def shards(
    S, X, Z,
    hidden_in, byte_qkv, byte_cache, byte_len, flags, coarse_prev, owner_map, up_weight,
    coarse_gain, query_weight, keyval_weight, return_weight, coarse_cache, coarse_len,
):
    T = X * Z
    part = up_weight.shape[1]
    gains = coarse_gain.reshape(T, part // HD, HD)
    owners = owner_map.transpose(1, 2, 0)
    rows = up_weight.shape[0] // S
    heads2 = 2 * HD
    vm = pl.BlockSpec(memory_space=pltpu.VMEM)
    hbm = pl.BlockSpec(memory_space=pl.ANY)
    dma = pltpu.SemaphoreType.DMA
    pair = lambda *shape: [dma(shape), dma(shape)]
    scratch = [
        pltpu.SMEM((1, 1), I32),
        pltpu.SMEM(flags.shape, I32),
        pltpu.VMEM(hidden_in.shape, BF16),
        pltpu.VMEM(byte_qkv.shape, BF16),
        pltpu.VMEM(coarse_prev.shape, BF16),
        pltpu.VMEM((S, T), I32),
        pltpu.VMEM(gains.shape[1:], F32),
        pltpu.VMEM(coarse_len.shape, I32),
        pltpu.VMEM((rows, part), BF16),
        pltpu.VMEM(byte_cache.shape[1:], BF16),
        pltpu.VMEM(up_weight.shape, BF16),
        pltpu.VMEM(query_weight.shape, BF16),
        pltpu.VMEM(keyval_weight.shape, BF16),
        pltpu.VMEM(return_weight.shape, BF16),
        pltpu.VMEM((coarse_cache.shape[1], coarse_cache.shape[3], HD), BF16),
        pltpu.VMEM((coarse_cache.shape[1], coarse_cache.shape[3], HD), BF16),
        pltpu.VMEM((32, HD), F32),
        pltpu.VMEM((4, 16, HD), F32),
        pltpu.VMEM((32, HD), F32),
        pltpu.VMEM((16, 256), F32),
        pltpu.VMEM((T * 8, HD), F32),
        pltpu.VMEM((T * 8, HD), F32),
        pltpu.VMEM((S, 16, 256 + HD), BF16),
        pltpu.VMEM((T, 16, 512), BF16),
        pltpu.VMEM((T, rows, part), BF16),
        pltpu.VMEM((S, rows, HD), BF16),
        pltpu.VMEM((S, rows, heads2), BF16),
        pltpu.VMEM((X, rows, heads2), BF16),
        pltpu.VMEM((X, rows, heads2), BF16),
        pltpu.VMEM((Z, rows // (8 * Z), 16, HD), BF16),
        pltpu.VMEM((Z, rows // (8 * Z), 16, HD), BF16),
        pltpu.VMEM((Z, rows // (8 * Z), 16, HD), BF16),
        pltpu.VMEM((Z, 8, T * 8), F32),
        pltpu.VMEM((X, 8, T * 8), F32),
        pltpu.VMEM((X, Z * 8, 1024), BF16),
        pltpu.VMEM((X, Z * 8, 1024), BF16),
        pltpu.VMEM((Z, 16, 512), BF16),
        pltpu.VMEM((Z, 16, 512), BF16),
        pltpu.VMEM((S, 16, 512), BF16),
        dma((16,)),
    ]
    Y = S // 2
    on_streams = [dma((Y,)), dma((Y,)), dma((2, 1)), dma((2, 1))]
    on_tp = [dma((Z,)), dma((Z,)), dma((X, Z)), dma((X, Z))]
    scratch += [on_streams, on_tp, on_tp] + [on_streams] * 3
    for shape in ((X,), (Z,), (Z,), (Z,), (X,), (X,), (Z,)):
        scratch += pair(*shape)
    return pl.pallas_call(
        functools.partial(kernel, S, X, Z),
        out_shape=jax.ShapeDtypeStruct(hidden_in.shape, BF16),
        in_specs=[hbm] * 14,
        out_specs=vm,
        scratch_shapes=scratch,
        compiler_params=pltpu.CompilerParams(
            collective_id=0, has_side_effects=True, vmem_limit_bytes=60 * 1024 * 1024
        ),
        name="decode",
    )(
        byte_len.reshape(1, 1), flags, hidden_in, byte_qkv, coarse_prev, owners, gains, coarse_len,
        byte_cache, up_weight, query_weight, keyval_weight, return_weight, coarse_cache,
    )


def solution(mesh):
    S, T = mesh.shape["streams"], mesh.shape["tp"]
    X = 4 if T >= 16 else 2
    return jax.shard_map(
        functools.partial(shards, S, X, T // X),
        mesh=mesh,
        in_specs=(
            P(("streams", "tp"), None, None),
            P(("streams", "tp"), None, None),
            P(("streams", "tp"), None, None),
            P(("streams", "tp")),
            P(("streams", "tp"), None),
            P(("streams", "tp"), None),
            P(),
            P(None, "tp"),
            P(),
            P(None, "tp"),
            P("tp", None),
            P("tp", None),
            P("streams", None, "tp", None, None),
            P("streams", None),
        ),
        out_specs=P(("streams", "tp"), None, None),
        check_vma=False,
    )
```

```python
import functools

import jax
import jax.numpy as jnp
from jax import lax
from jax.experimental import pallas as pl
from jax.experimental.pallas import tpu as pltpu
from jax.sharding import PartitionSpec as P

HD = 128
EPSILON = 1e-05
NEG_FILL = -1e30
F32, BF16, I32 = jnp.float32, jnp.bfloat16, jnp.int32
MESH = pl.DeviceIdType.MESH


def iota(shape, dim):
    return lax.broadcasted_iota(I32, shape, dim)


def dot(a, b):
    return lax.dot_general(a, b, (((1,), (0,)), ((), ())), preferred_element_type=F32)


def dot_t(a, b):
    return lax.dot_general(a, b, (((1,), (1,)), ((), ())), preferred_element_type=F32)


def bdot(a, b):
    return lax.dot_general(a, b, (((2,), (1,)), ((0,), (0,))), preferred_element_type=F32)


def bdot_t(a, b):
    return lax.dot_general(a, b, (((2,), (2,)), ((0,), (0,))), preferred_element_type=F32)


def kernel(
    S, X, Z,
    byte_len_hbm, flags_hbm, hidden_hbm, qkv_hbm, prev_hbm, owner_hbm, gain_hbm, len_hbm,
    byte_cache, up_hbm, query_hbm, keyval_hbm, return_hbm, cache_hbm,
    out_ref,
    byte_len, flags, hidden, qkv, prev, owners, gain, coarse_len,
    first, bc, up, wq, wkv, wr, ck, cv,
    qs, kn, os, xm, raw, cols,
    XS, XT, UT, MQ, MK, KP, KX, KS, KZ, KA, SQZ, SQX, PX, RX, PZ, RZ, RB,
    local_sem,
    xs_sems, xt_sems, ut_sems, mq_sems, mk_sems, rb_sems,
    kx_s, kx_r, kz_s, kz_r, ka_s, ka_r, sqz_s, sqz_r, sqx_s, sqx_r,
    px_s, px_r, pz_s, pz_r,
):
    T = X * Z
    me_s, me_t = lax.axis_index("streams"), lax.axis_index("tp")
    x, z = me_t // Z, me_t % Z
    Y = S // 2
    y, core = me_s // 2, me_s % 2
    me_p = core * Y + y
    rows_own = first.shape[0]

    small = [
        pltpu.make_async_copy(gain_hbm.at[me_t], gain, local_sem.at[6]),
        pltpu.make_async_copy(hidden_hbm, hidden, local_sem.at[7]),
        pltpu.make_async_copy(qkv_hbm, qkv, local_sem.at[8]),
        pltpu.make_async_copy(prev_hbm, prev, local_sem.at[9]),
        pltpu.make_async_copy(owner_hbm.at[:, 0, :], owners, local_sem.at[10]),
        pltpu.make_async_copy(len_hbm, coarse_len, local_sem.at[11]),
        pltpu.make_async_copy(byte_len_hbm, byte_len, local_sem.at[12]),
        pltpu.make_async_copy(flags_hbm, flags, local_sem.at[13]),
    ]
    locals_ = [
        pltpu.make_async_copy(up_hbm, up, local_sem.at[0]),
        pltpu.make_async_copy(byte_cache.at[0], bc, local_sem.at[1]),
        pltpu.make_async_copy(keyval_hbm, wkv, local_sem.at[2]),
        pltpu.make_async_copy(query_hbm, wq, local_sem.at[3]),
        pltpu.make_async_copy(cache_hbm.at[0, :, 0, :, pl.ds(0, HD)], ck, local_sem.at[4]),
        pltpu.make_async_copy(return_hbm, wr, local_sem.at[5]),
        pltpu.make_async_copy(cache_hbm.at[0, :, 0, :, pl.ds(HD, HD)], cv, local_sem.at[14]),
    ]
    own_up = pltpu.make_async_copy(
        up_hbm.at[pl.ds(pl.multiple_of(me_p * rows_own, rows_own), rows_own)], first, local_sem.at[15])
    own_up.start()
    for copy in small + [locals_[2], locals_[1]]:
        copy.start()

    def y_peer(d):
        return (lax.rem(y + d, Y) * 2 + core, me_t)

    def core_peer(d):
        return (y * 2 + lax.rem(core + d, 2), me_t)

    def z_peer(d):
        return (me_s, x * Z + lax.rem(z + d, Z))

    def x_peer(d):
        return (me_s, lax.rem(x + d, X) * Z + z)

    def loop(count, body):
        def step(d, carry):
            body(d)
            return carry

        lax.fori_loop(1, count, step, 0)

    def remote(src, dst, send, recv, peer):
        return pltpu.make_async_remote_copy(
            src_ref=src, dst_ref=dst, send_sem=send, recv_sem=recv,
            device_id=peer, device_id_type=MESH,
        )

    barrier = pltpu.get_barrier_semaphore()
    for count, peer in ((Y, y_peer), (2, core_peer), (Z, z_peer), (X, x_peer)):
        loop(count, lambda d, peer=peer: pl.semaphore_signal(
            barrier, inc=1, device_id=peer(d), device_id_type=MESH))

    def far_first(count):
        return sorted(range(1, count), key=lambda d: -min(d, count - d))

    comms = []

    class Axis:
        def __init__(self, src, dst, me, count, peer, send, recv):
            self.src, self.dst, self.me, self.count = src, dst, me, count
            self.peer, self.send, self.recv_sem = peer, send, recv
            self.received = False
            comms.append(self)

        def copy(self, d, src, dst):
            return remote(src, dst, self.send.at[d], self.recv_sem.at[d], self.peer(d))

        def start(self):
            def body(d):
                other = self.me if self.src is self.dst else lax.rem(self.me + d, self.count)
                self.copy(d, self.src.at[other], self.dst.at[self.me]).start()

            loop(self.count, body)
            return self

        def recv(self):
            def body(d):
                block = self.dst.at[lax.rem(self.me + self.count - d, self.count)]
                self.copy(d, block, block).wait_recv()

            loop(self.count, body)
            self.received = True

        def total(self, own_part):
            if not self.received:
                self.recv()
            total = own_part.astype(F32)
            for d in range(1, self.count):
                total = total + self.dst[lax.rem(self.me + self.count - d, self.count)].astype(F32)
            return total

        def finish(self):
            if not self.received:
                self.recv()
            loop(self.count, lambda d: self.copy(d, self.dst.at[0], self.dst.at[0]).wait_send())

    class Plane:
        def __init__(self, buf, first, second, sems, whole):
            self.buf, self.whole = buf, whole
            (self.me1, self.n1, self.peer1), (self.me2, self.n2, self.peer2) = first, second
            self.s1, self.r1, self.s2, self.r2 = sems
            self.forwarded, self.got = False, set()
            comms.append(self)

        def place(self, i, j):
            return j * self.n1 + i

        def line(self, d, j):
            group = self.buf.at[pl.ds(j * self.n1, self.n1)]
            return remote(group, group, self.s2.at[d, 0], self.r2.at[d, 0], self.peer2(d))

        def hop1(self, d, block):
            return remote(block, block, self.s1.at[d], self.r1.at[d], self.peer1(d))

        def hop2(self, d, i, block):
            return remote(block, block, self.s2.at[d, i], self.r2.at[d, i], self.peer2(d))

        def onward(self, i):
            block = self.buf.at[self.place(i, self.me2)]
            for d in far_first(self.n2):
                self.hop2(d, i, block).start()

        def start(self):
            block = self.buf.at[self.place(self.me1, self.me2)]
            if not self.whole:
                self.onward(self.me1)
            loop(self.n1, lambda d: self.hop1(d, block).start())
            return self

        def forward(self):
            def body(d):
                i = lax.rem(self.me1 + self.n1 - d, self.n1)
                self.hop1(d, self.buf.at[self.place(i, self.me2)]).wait_recv()
                if not self.whole:
                    self.onward(i)

            loop(self.n1, body)
            if self.whole:
                loop(self.n2, lambda d: self.line(d, self.me2).start())
            self.forwarded = True

        def each(self, body):
            def step(i, carry):
                body(i)
                return carry

            lax.fori_loop(0, self.n1, step, 0)

        def arrived(self, d):
            source = lax.rem(self.me2 + self.n2 - d, self.n2)
            if self.whole:
                self.line(d, source).wait_recv()
            else:
                self.each(
                    lambda i: self.hop2(d, i, self.buf.at[self.place(i, source)]).wait_recv())
            self.got.add(d)

        def recv(self):
            if not self.forwarded:
                self.forward()
            for d in range(1, self.n2):
                if d not in self.got:
                    self.arrived(d)

        def finish(self):
            self.recv()
            block = self.buf.at[0]
            loop(self.n1, lambda d: self.hop1(d, block).wait_send())
            if self.whole:
                loop(self.n2, lambda d: self.line(d, 0).wait_send())
            else:
                self.each(lambda i: loop(self.n2, lambda d: self.hop2(d, i, block).wait_send()))

    def over_tp(buf, sems, whole):
        return Plane(buf, (z, Z, z_peer), (x, X, x_peer), sems, whole)

    def over_streams(buf, sems):
        return Plane(buf, (y, Y, y_peer), (core, 2, core_peer), sems, True)

    small[0].wait()
    own_up.wait()
    gain_row = jnp.concatenate([gain[0:1, :], gain[1:2, :]], axis=1)
    UT[me_t] = (first[...].astype(F32) * gain_row).astype(BF16)
    pl.semaphore_wait(barrier, Y + Z + X - 2)
    ups = over_tp(UT, ut_sems, False).start()
    for copy in (locals_[0], locals_[3], locals_[4], locals_[6], locals_[5]):
        copy.start()

    locals_[2].wait()
    kv_heads = wkv.shape[1] // (2 * HD)
    partial = dot(UT[me_t], wkv[...]).astype(BF16)
    for j in range(kv_heads):
        KP[j] = jnp.concatenate(
            [partial[:, j * HD:(j + 1) * HD], partial[:, (kv_heads + j) * HD:(kv_heads + j + 1) * HD]],
            axis=1,
        )
    kv_x = Axis(KP, KX, x, X, x_peer, kx_s, kx_r).start()

    for copy in small[1:]:
        copy.wait()
    steps = hidden.shape[1]
    lanes = iota((16, HD), 1)
    marks = jnp.zeros((16, HD), F32)
    last = jnp.int32(-1)
    step_of_row = iota((16, 1), 0) % 4
    last_col = jnp.full((16, 1), -1, I32)
    for u in range(steps):
        mark = flags[0, u]
        marks = marks + jnp.where(lanes % 4 == u, mark.astype(F32), 0.0)
        last = jnp.where(mark > 0, jnp.int32(u), last)
        last_col = jnp.where(step_of_row == u, last, last_col)

    locals_[1].wait()
    kn[...] = jnp.zeros_like(kn)
    for i in range(2):
        for hh in range(4):
            qs[pl.ds(i * 16 + hh * 4, 4), :] = qkv[0, :, pl.ds((i * 4 + hh) * HD, HD)].astype(F32)
        kn[i, 0:4, :] = qkv[0, :, pl.ds((8 + i) * HD, HD)].astype(F32)
        kn[2 + i, 0:4, :] = qkv[0, :, pl.ds((10 + i) * HD, HD)].astype(F32)
    length = bc.shape[0]
    scaling = HD ** (-0.5)
    seen = iota((16, length), 1) < byte_len[0, 0]
    causal = iota((16, 16), 1) <= iota((16, 16), 0) % 4
    for i in range(2):
        q_i = qs[pl.ds(i * 16, 16), :].astype(BF16)
        old = dot_t(q_i, bc[:, pl.ds(i * HD, HD)]) * scaling
        old = jnp.where(seen, old, NEG_FILL)
        new = dot_t(q_i, kn[i].astype(BF16)) * scaling
        new = jnp.where(causal, new, NEG_FILL)
        top = jnp.maximum(jnp.max(old, axis=1, keepdims=True), jnp.max(new, axis=1, keepdims=True))
        old, new = jnp.exp(old - top), jnp.exp(new - top)
        total = jnp.sum(old, axis=1, keepdims=True) + jnp.sum(new, axis=1, keepdims=True)
        old, new = (old / total).astype(BF16), (new / total).astype(BF16)
        os[pl.ds(i * 16, 16), :] = dot(old, bc[:, pl.ds((2 + i) * HD, HD)]) + dot(
            new, kn[2 + i].astype(BF16))
        for hh in range(4):
            xm[pl.ds((2 * i + hh // 2) * 4, 4), pl.ds((hh % 2) * HD, HD)] = (
                hidden[0, :, pl.ds((i * 4 + hh) * HD, HD)].astype(F32) + os[pl.ds(i * 16 + hh * 4, 4), :]
            )
    rows_16 = xm[...].astype(BF16)
    XS[me_p] = jnp.concatenate([rows_16, marks.astype(BF16)], axis=1)
    rows_s = over_streams(XS, xs_sems).start()

    ups.forward()
    rows_s.forward()

    tiles = kv_x.total(KP[x]).astype(BF16)
    tall = rows_own // 16
    for b in range(2 * tall):
        KS[b // (2 * tall // Z), b % (2 * tall // Z)] = tiles[
            (b // 2) * 16:(b // 2 + 1) * 16, (b % 2) * HD:(b % 2 + 1) * HD]
    kv_z = Axis(KS, KZ, z, Z, z_peer, kz_s, kz_r).start()

    o_col = jnp.sum(
        jnp.where(iota((S, T), 1) == me_t, owners[...].astype(F32), 0.0), axis=1, keepdims=True)
    eye = iota((S, S), 0) == iota((S, S), 1)
    o_row = jnp.sum(jnp.where(eye, o_col, 0.0), axis=0, keepdims=True)
    same = o_col == o_row
    rank_col = jnp.sum(
        jnp.where(same & (iota((S, S), 1) < iota((S, S), 0)), 1.0, 0.0), axis=1, keepdims=True)
    own_col = iota((S, 1), 0) == me_s
    my_owner = jnp.sum(jnp.where(own_col, o_col, 0.0), axis=0, keepdims=True)
    my_rank = jnp.sum(jnp.where(own_col, rank_col, 0.0), axis=0, keepdims=True)
    tgt_col = jnp.where(o_col == me_s.astype(F32), rank_col, -1.0)
    W = S * 16
    stream_of = lambda lane: (lane // 16 % Y) * 2 + lane // (16 * Y)
    tgt = jnp.sum(
        jnp.where(stream_of(iota((S, W), 1)) == iota((S, W), 0), tgt_col, 0.0), axis=0, keepdims=True)

    rows_s.recv()
    r, l = iota((16, W), 0), iota((16, W), 1)
    every = XS[...].reshape(W, 256 + HD)
    picked = (tgt == ((r % 8) // 4).astype(F32)) & (l % 4 == r % 4)
    halves = []
    for part in range(2):
        pick = jnp.where(picked & ((l % 16) // 4 == (r // 8) * 2 + part), 1.0, 0.0).astype(BF16)
        halves.append(dot(pick, every[:, :256]).astype(BF16))
    XT[me_t] = jnp.concatenate(halves, axis=1)
    rows_t = over_tp(XT, xt_sems, True).start()
    slot_marks = []
    for j in range(2):
        pick = jnp.where((tgt == float(j)) & (l % 16 == 0), 1.0, 0.0).astype(BF16)
        slot_marks.append(dot(pick, every[:, 256:]))
    slot_marks = jnp.where((lanes % 8) // 4 == 0, slot_marks[0], slot_marks[1])[0:8, :]

    locals_[3].wait()

    def query_part(source, total):
        base = pl.multiple_of(source * (Z * 256), Z * 256)
        for zb in range(Z):
            total = total + dot(UT[source * Z + zb], wq[pl.ds(base + zb * 256, 256), :])
        return total

    folded = query_part(x, jnp.zeros((rows_own, HD), F32))
    KA[z] = kv_z.total(KS[z]).astype(BF16)
    kv_all = Axis(KA, KA, z, Z, z_peer, ka_s, ka_r).start()
    rows_t.forward()
    for d in range(1, X):
        ups.arrived(d)
        folded = query_part(lax.rem(x + X - d, X), folded)
        if d == 1:
            kv_all.recv()
            for b in range(2 * tall):
                MK[me_p, pl.ds((b // 2) * 16, 16), pl.ds((b % 2) * HD, HD)] = KA[
                    b // (2 * tall // Z), b % (2 * tall // Z)]
            keyvals_s = over_streams(MK, mk_sems).start()
    MQ[me_p] = folded.astype(BF16)
    queries_s = over_streams(MQ, mq_sems).start()

    locals_[0].wait()
    rows_t.recv()
    rows_all = XT[...].reshape(T * 16, 512)
    N = T * 8

    def project(top, bottom, width):
        upper = dot(rows_all, top).reshape(T, 16, width)[:, :8]
        lower = dot(rows_all, bottom).reshape(T, 16, width)[:, 8:]
        return (upper + lower).reshape(N, width)

    expanded = project(up[0:512, :], up[512:1024, :], up.shape[1]).astype(BF16).astype(F32)
    squared = expanded * expanded
    high = squared.astype(BF16)
    low = (squared - high.astype(F32)).astype(BF16)
    ones = jnp.ones((8, up.shape[1]), BF16)
    spot = slot_marks[:, :N] if N <= HD else jnp.concatenate([slot_marks] * (N // HD), axis=1)
    spot = jnp.where(iota((8, N), 1) // 8 == me_t, spot, 0.0)
    SQZ[z] = jnp.where(iota((8, N), 0) == 0, dot_t(ones, high) + dot_t(ones, low), spot)
    squares_z = Axis(SQZ, SQZ, z, Z, z_peer, sqz_s, sqz_r).start()
    keyvals_s.forward()
    queries_s.forward()
    SQX[x] = squares_z.total(SQZ[z])
    squares_x = Axis(SQX, SQX, x, X, x_peer, sqx_s, sqx_r).start()

    keyvals_s.recv()
    weights = MK[...].reshape(S * rows_own, 2 * HD)
    keyvals = project(weights[:512], weights[512:], 2 * HD)
    keys = keyvals[:, :HD].astype(BF16)
    queries_s.recv()
    weights = MQ[...].reshape(S * rows_own, HD)
    raw[...] = project(weights[:512], weights[512:], HD)

    locals_[4].wait()
    locals_[6].wait()
    locals_[5].wait()
    slots, span = ck.shape[0], ck.shape[1]
    len_col = jnp.sum(
        jnp.where(iota((N, slots), 0) // 4 == iota((N, slots), 1), coarse_len[...].astype(F32), 0.0),
        axis=1, keepdims=True)
    summed = squares_x.total(SQX[x])
    inverse_row = lax.rsqrt(summed[0:1, :] / (up.shape[1] * T) + EPSILON)
    marked = summed[1:2, :] > 0.5
    inverse = jnp.sum(
        jnp.where(iota((N, N), 0) == iota((N, N), 1), inverse_row, 0.0), axis=1, keepdims=True)
    cols[...] = jnp.where(iota((N, HD), 1) == 0, inverse, len_col)
    values = (keyvals[:, HD:] * inverse).astype(BF16)

    block, per = Z * 8, min(8, Z * 2)
    chunks = Z * 2 // per
    by_chunk = lambda col: col.reshape(chunks, per * 4, 1)
    row_old, lane_old = iota((per * 4, per * span), 0), iota((per * 4, per * span), 1)
    position = jnp.where(lane_old // span == row_old // 4, lane_old % span, span).astype(F32)
    lane_new, row_new = iota((block, N), 1), iota((block, N), 0)
    back_x = Axis(PX, RX, x, X, x_peer, px_s, px_r)
    for d in far_first(X) + [0]:
        to = lax.rem(x + d, X)
        at_row = pl.ds(pl.multiple_of(to * block, block), block)
        at_slot = pl.ds(to * (Z * 2), Z * 2)
        queries = raw[at_row, :].astype(BF16)
        factor, filled = cols[at_row, 0:1] * scaling, cols[at_row, 1:2]
        old = bdot_t(queries.reshape(chunks, per * 4, HD), ck[at_slot].reshape(chunks, per * span, HD))
        new = dot_t(queries, keys)
        row = row_new + to * block
        allowed = (lane_new // 4 == row // 4) & (lane_new % 4 <= row % 4) & marked
        old = jnp.where(position[None] < by_chunk(filled), old * by_chunk(factor), NEG_FILL)
        new = jnp.where(allowed, new * factor * inverse_row, NEG_FILL)
        top = jnp.maximum(
            jnp.max(old, axis=2, keepdims=True).reshape(block, 1), jnp.max(new, axis=1, keepdims=True))
        old, new = jnp.exp(old - by_chunk(top)), jnp.exp(new - top)
        total = jnp.sum(old, axis=2, keepdims=True).reshape(block, 1) + jnp.sum(
            new, axis=1, keepdims=True)
        old, new = (old / by_chunk(total)).astype(BF16), (new / total).astype(BF16)
        attended = bdot(old, cv[at_slot].reshape(chunks, per * span, HD)).reshape(block, HD)
        attended = (attended + dot(new, values)).astype(BF16)
        PX[to] = dot(attended, wr[...]).astype(BF16)
        if d:
            back_x.copy(d, PX.at[to], RX.at[x]).start()

    for comm in comms:
        if comm is not back_x:
            comm.finish()

    summed = back_x.total(PX[x]).reshape(Z, 8, 1024)
    PZ[...] = jnp.concatenate([summed[:, :, :512], summed[:, :, 512:]], axis=1).astype(BF16)
    back_z = Axis(PZ, RZ, z, Z, z_peer, pz_s, pz_r).start()
    RB[me_p] = back_z.total(PZ[z]).astype(BF16)
    back_s = over_streams(RB, rb_sems).start()
    back_s.recv()

    home = (stream_of(l).astype(F32) == my_owner) & (((l % 8) // 4).astype(F32) == my_rank)
    home = home & (l % 4 == last_col) & ((l % 16) // 8 == r // 8)
    back = RB[...].reshape(W, 512)
    latest = jnp.zeros((16, 256), F32)
    for part in range(2):
        pick = jnp.where(home & ((r // 4) % 2 == part), 1.0, 0.0).astype(BF16)
        latest = latest + dot(pick, back[:, part * 256:(part + 1) * 256])
    earlier = jnp.zeros((16, 256), F32)
    for k in range(4):
        earlier = jnp.where(
            iota((16, 256), 0) // 4 == k, prev[0:1, pl.ds(k * 256, 256)].astype(F32), earlier)
    latest = jnp.where(last_col < 0, earlier, latest)
    xm[...] = rows_16.astype(F32) + latest
    for k in range(4):
        out_ref[0, :, pl.ds(k * 256, 256)] = xm[pl.ds(k * 4, 4), :].astype(BF16)

    for comm in (back_x, back_z, back_s):
        comm.finish()


def shards(
    S, X, Z,
    hidden_in, byte_qkv, byte_cache, byte_len, flags, coarse_prev, owner_map, up_weight,
    coarse_gain, query_weight, keyval_weight, return_weight, coarse_cache, coarse_len,
):
    T = X * Z
    part = up_weight.shape[1]
    gains = coarse_gain.reshape(T, part // HD, HD)
    owners = owner_map.transpose(1, 2, 0)
    rows = up_weight.shape[0] // S
    heads2 = 2 * HD
    vm = pl.BlockSpec(memory_space=pltpu.VMEM)
    dma = pltpu.SemaphoreType.DMA
    pair = lambda *shape: [dma(shape), dma(shape)]
    scratch = [
        pltpu.SMEM((1, 1), I32),
        pltpu.SMEM(flags.shape, I32),
        pltpu.VMEM(hidden_in.shape, BF16),
        pltpu.VMEM(byte_qkv.shape, BF16),
        pltpu.VMEM(coarse_prev.shape, BF16),
        pltpu.VMEM((S, T), I32),
        pltpu.VMEM(gains.shape[1:], F32),
        pltpu.VMEM(coarse_len.shape, I32),
        pltpu.VMEM((rows, part), BF16),
        pltpu.VMEM(byte_cache.shape[1:], BF16),
        pltpu.VMEM(up_weight.shape, BF16),
        pltpu.VMEM(query_weight.shape, BF16),
        pltpu.VMEM(keyval_weight.shape, BF16),
        pltpu.VMEM(return_weight.shape, BF16),
        pltpu.VMEM((coarse_cache.shape[1], coarse_cache.shape[3], HD), BF16),
        pltpu.VMEM((coarse_cache.shape[1], coarse_cache.shape[3], HD), BF16),
        pltpu.VMEM((32, HD), F32),
        pltpu.VMEM((4, 16, HD), F32),
        pltpu.VMEM((32, HD), F32),
        pltpu.VMEM((16, 256), F32),
        pltpu.VMEM((T * 8, HD), F32),
        pltpu.VMEM((T * 8, HD), F32),
        pltpu.VMEM((S, 16, 256 + HD), BF16),
        pltpu.VMEM((T, 16, 512), BF16),
        pltpu.VMEM((T, rows, part), BF16),
        pltpu.VMEM((S, rows, HD), BF16),
        pltpu.VMEM((S, rows, heads2), BF16),
        pltpu.VMEM((X, rows, heads2), BF16),
        pltpu.VMEM((X, rows, heads2), BF16),
        pltpu.VMEM((Z, rows // (8 * Z), 16, HD), BF16),
        pltpu.VMEM((Z, rows // (8 * Z), 16, HD), BF16),
        pltpu.VMEM((Z, rows // (8 * Z), 16, HD), BF16),
        pltpu.VMEM((Z, 8, T * 8), F32),
        pltpu.VMEM((X, 8, T * 8), F32),
        pltpu.VMEM((X, Z * 8, 1024), BF16),
        pltpu.VMEM((X, Z * 8, 1024), BF16),
        pltpu.VMEM((Z, 16, 512), BF16),
        pltpu.VMEM((Z, 16, 512), BF16),
        pltpu.VMEM((S, 16, 512), BF16),
        dma((16,)),
    ]
    Y = S // 2
    on_streams = [dma((Y,)), dma((Y,)), dma((2, 1)), dma((2, 1))]
    on_tp = [dma((Z,)), dma((Z,)), dma((X, Z)), dma((X, Z))]
    scratch += [on_streams, on_tp, on_tp] + [on_streams] * 3
    for shape in ((X,), (Z,), (Z,), (Z,), (X,), (X,), (Z,)):
        scratch += pair(*shape)
    return pl.pallas_call(
        functools.partial(kernel, S, X, Z),
        out_shape=jax.ShapeDtypeStruct(hidden_in.shape, BF16),
        in_specs=[pl.BlockSpec(memory_space=pltpu.HBM)] * 14,
        out_specs=vm,
        scratch_shapes=scratch,
        compiler_params=pltpu.CompilerParams(
            collective_id=0, has_side_effects=True, vmem_limit_bytes=60 * 1024 * 1024
        ),
        name="decode",
    )(
        byte_len.reshape(1, 1), flags, hidden_in, byte_qkv, coarse_prev, owners, gains, coarse_len,
        byte_cache, up_weight, query_weight, keyval_weight, return_weight, coarse_cache,
    )


def solution(mesh):
    S, T = mesh.shape["streams"], mesh.shape["tp"]
    X = 4 if T >= 16 else 2
    return jax.shard_map(
        functools.partial(shards, S, X, T // X),
        mesh=mesh,
        in_specs=(
            P(("streams", "tp"), None, None),
            P(("streams", "tp"), None, None),
            P(("streams", "tp"), None, None),
            P(("streams", "tp")),
            P(("streams", "tp"), None),
            P(("streams", "tp"), None),
            P(),
            P(None, "tp"),
            P(),
            P(None, "tp"),
            P("tp", None),
            P("tp", None),
            P("streams", None, "tp", None, None),
            P("streams", None),
        ),
        out_specs=P(("streams", "tp"), None, None),
        check_vma=False,
    )
```

```python
import functools

import jax
import jax.numpy as jnp
from jax import lax
from jax.experimental import pallas as pl
from jax.experimental.pallas import tpu as pltpu
from jax.sharding import PartitionSpec as P

HD = 128
EPSILON = 1e-05
NEG_FILL = -1e30
F32, BF16, I32 = jnp.float32, jnp.bfloat16, jnp.int32
MESH = pl.DeviceIdType.MESH


def iota(shape, dim):
    return lax.broadcasted_iota(I32, shape, dim)


def dot(a, b):
    return lax.dot_general(a, b, (((1,), (0,)), ((), ())), preferred_element_type=F32)


def dot_t(a, b):
    return lax.dot_general(a, b, (((1,), (1,)), ((), ())), preferred_element_type=F32)


def bdot(a, b):
    return lax.dot_general(a, b, (((2,), (1,)), ((0,), (0,))), preferred_element_type=F32)


def bdot_t(a, b):
    return lax.dot_general(a, b, (((2,), (2,)), ((0,), (0,))), preferred_element_type=F32)


def kernel(
    S, X, Z,
    byte_len_hbm, flags_hbm, hidden_hbm, qkv_hbm, prev_hbm, owner_hbm, gain_hbm, len_hbm,
    byte_cache, up_hbm, query_hbm, keyval_hbm, return_hbm, cache_hbm,
    out_ref,
    byte_len, flags, hidden, qkv, prev, owners, gain, coarse_len,
    first, bc, up, wq, wkv, wr, ck, cv,
    qs, kn, os, xm, raw, cols,
    XS, XT, UT, MQ, MK, KP, KX, KS, KZ, KA, SQZ, SQX, PX, RX, PZ, RZ, RB,
    local_sem,
    xs_sems, xt_sems, ut_sems, mq_sems, mk_sems, rb_sems,
    kx_s, kx_r, kz_s, kz_r, ka_s, ka_r, sqz_s, sqz_r, sqx_s, sqx_r,
    px_s, px_r, pz_s, pz_r,
):
    T = X * Z
    me_s, me_t = lax.axis_index("streams"), lax.axis_index("tp")
    x, z = me_t // Z, me_t % Z
    Y = S // 2
    y, core = me_s // 2, me_s % 2
    me_p = core * Y + y
    rows_own = first.shape[0]

    small = [
        pltpu.make_async_copy(gain_hbm.at[me_t], gain, local_sem.at[6]),
        pltpu.make_async_copy(hidden_hbm, hidden, local_sem.at[7]),
        pltpu.make_async_copy(qkv_hbm, qkv, local_sem.at[8]),
        pltpu.make_async_copy(prev_hbm, prev, local_sem.at[9]),
        pltpu.make_async_copy(owner_hbm.at[:, 0, :], owners, local_sem.at[10]),
        pltpu.make_async_copy(len_hbm, coarse_len, local_sem.at[11]),
        pltpu.make_async_copy(byte_len_hbm, byte_len, local_sem.at[12]),
        pltpu.make_async_copy(flags_hbm, flags, local_sem.at[13]),
    ]
    locals_ = [
        pltpu.make_async_copy(up_hbm, up, local_sem.at[0]),
        pltpu.make_async_copy(byte_cache.at[0], bc, local_sem.at[1]),
        pltpu.make_async_copy(keyval_hbm, wkv, local_sem.at[2]),
        pltpu.make_async_copy(query_hbm, wq, local_sem.at[3]),
        pltpu.make_async_copy(cache_hbm.at[0, :, 0, :, pl.ds(0, HD)], ck, local_sem.at[4]),
        pltpu.make_async_copy(return_hbm, wr, local_sem.at[5]),
        pltpu.make_async_copy(cache_hbm.at[0, :, 0, :, pl.ds(HD, HD)], cv, local_sem.at[14]),
    ]
    own_up = pltpu.make_async_copy(
        up_hbm.at[pl.ds(pl.multiple_of(me_p * rows_own, rows_own), rows_own)], first, local_sem.at[15])
    own_up.start()
    for copy in small + [locals_[2], locals_[1]]:
        copy.start()

    def y_peer(d):
        return (lax.rem(y + d, Y) * 2 + core, me_t)

    def core_peer(d):
        return (y * 2 + lax.rem(core + d, 2), me_t)

    def z_peer(d):
        return (me_s, x * Z + lax.rem(z + d, Z))

    def x_peer(d):
        return (me_s, lax.rem(x + d, X) * Z + z)

    def loop(count, body):
        for d in range(1, count):
            body(d)

    def remote(src, dst, send, recv, peer):
        return pltpu.make_async_remote_copy(
            src_ref=src, dst_ref=dst, send_sem=send, recv_sem=recv,
            device_id=peer, device_id_type=MESH,
        )

    barrier = pltpu.get_barrier_semaphore()
    for count, peer in ((Y, y_peer), (2, core_peer), (Z, z_peer), (X, x_peer)):
        loop(count, lambda d, peer=peer: pl.semaphore_signal(
            barrier, inc=1, device_id=peer(d), device_id_type=MESH))

    def far_first(count):
        return sorted(range(1, count), key=lambda d: -min(d, count - d))

    comms = []

    class Axis:
        def __init__(self, src, dst, me, count, peer, send, recv):
            self.src, self.dst, self.me, self.count = src, dst, me, count
            self.peer, self.send, self.recv_sem = peer, send, recv
            self.received = False
            comms.append(self)

        def copy(self, d, src, dst):
            return remote(src, dst, self.send.at[d], self.recv_sem.at[d], self.peer(d))

        def start(self):
            def body(d):
                other = self.me if self.src is self.dst else lax.rem(self.me + d, self.count)
                self.copy(d, self.src.at[other], self.dst.at[self.me]).start()

            loop(self.count, body)
            return self

        def recv(self):
            def body(d):
                block = self.dst.at[lax.rem(self.me + self.count - d, self.count)]
                self.copy(d, block, block).wait_recv()

            loop(self.count, body)
            self.received = True

        def total(self, own_part):
            if not self.received:
                self.recv()
            total = own_part.astype(F32)
            for d in range(1, self.count):
                total = total + self.dst[lax.rem(self.me + self.count - d, self.count)].astype(F32)
            return total

        def finish(self):
            if not self.received:
                self.recv()
            loop(self.count, lambda d: self.copy(d, self.dst.at[0], self.dst.at[0]).wait_send())

    class Plane:
        def __init__(self, buf, first, second, sems, whole):
            self.buf, self.whole = buf, whole
            (self.me1, self.n1, self.peer1), (self.me2, self.n2, self.peer2) = first, second
            self.s1, self.r1, self.s2, self.r2 = sems
            self.forwarded, self.got = False, set()
            comms.append(self)

        def place(self, i, j):
            return j * self.n1 + i

        def line(self, d, j):
            group = self.buf.at[pl.ds(j * self.n1, self.n1)]
            return remote(group, group, self.s2.at[d, 0], self.r2.at[d, 0], self.peer2(d))

        def hop1(self, d, block):
            return remote(block, block, self.s1.at[d], self.r1.at[d], self.peer1(d))

        def hop2(self, d, i, block):
            return remote(block, block, self.s2.at[d, i], self.r2.at[d, i], self.peer2(d))

        def onward(self, i):
            block = self.buf.at[self.place(i, self.me2)]
            for d in far_first(self.n2):
                self.hop2(d, i, block).start()

        def start(self):
            block = self.buf.at[self.place(self.me1, self.me2)]
            if not self.whole:
                self.onward(self.me1)
            loop(self.n1, lambda d: self.hop1(d, block).start())
            return self

        def forward(self):
            def body(d):
                i = lax.rem(self.me1 + self.n1 - d, self.n1)
                self.hop1(d, self.buf.at[self.place(i, self.me2)]).wait_recv()
                if not self.whole:
                    self.onward(i)

            loop(self.n1, body)
            if self.whole:
                loop(self.n2, lambda d: self.line(d, self.me2).start())
            self.forwarded = True

        def each(self, body):
            def step(i, carry):
                body(i)
                return carry

            lax.fori_loop(0, self.n1, step, 0)

        def arrived(self, d):
            source = lax.rem(self.me2 + self.n2 - d, self.n2)
            if self.whole:
                self.line(d, source).wait_recv()
            else:
                self.each(
                    lambda i: self.hop2(d, i, self.buf.at[self.place(i, source)]).wait_recv())
            self.got.add(d)

        def recv(self):
            if not self.forwarded:
                self.forward()
            for d in range(1, self.n2):
                if d not in self.got:
                    self.arrived(d)

        def finish(self):
            self.recv()
            block = self.buf.at[0]
            loop(self.n1, lambda d: self.hop1(d, block).wait_send())
            if self.whole:
                loop(self.n2, lambda d: self.line(d, 0).wait_send())
            else:
                self.each(lambda i: loop(self.n2, lambda d: self.hop2(d, i, block).wait_send()))

    def over_tp(buf, sems, whole):
        return Plane(buf, (z, Z, z_peer), (x, X, x_peer), sems, whole)

    def over_streams(buf, sems):
        return Plane(buf, (y, Y, y_peer), (core, 2, core_peer), sems, True)

    small[0].wait()
    own_up.wait()
    gain_row = jnp.concatenate([gain[0:1, :], gain[1:2, :]], axis=1)
    UT[me_t] = (first[...].astype(F32) * gain_row).astype(BF16)
    pl.semaphore_wait(barrier, Y + Z + X - 2)
    ups = over_tp(UT, ut_sems, False).start()
    for copy in (locals_[0], locals_[3], locals_[4], locals_[6], locals_[5]):
        copy.start()

    locals_[2].wait()
    kv_heads = wkv.shape[1] // (2 * HD)
    partial = dot(UT[me_t], wkv[...]).astype(BF16)
    for j in range(kv_heads):
        KP[j] = jnp.concatenate(
            [partial[:, j * HD:(j + 1) * HD], partial[:, (kv_heads + j) * HD:(kv_heads + j + 1) * HD]],
            axis=1,
        )
    kv_x = Axis(KP, KX, x, X, x_peer, kx_s, kx_r).start()

    for copy in small[1:]:
        copy.wait()
    steps = hidden.shape[1]
    lanes = iota((16, HD), 1)
    marks = jnp.zeros((16, HD), F32)
    last = jnp.int32(-1)
    step_of_row = iota((16, 1), 0) % 4
    last_col = jnp.full((16, 1), -1, I32)
    for u in range(steps):
        mark = flags[0, u]
        marks = marks + jnp.where(lanes % 4 == u, mark.astype(F32), 0.0)
        last = jnp.where(mark > 0, jnp.int32(u), last)
        last_col = jnp.where(step_of_row == u, last, last_col)

    locals_[1].wait()
    kn[...] = jnp.zeros_like(kn)
    for i in range(2):
        for hh in range(4):
            qs[pl.ds(i * 16 + hh * 4, 4), :] = qkv[0, :, pl.ds((i * 4 + hh) * HD, HD)].astype(F32)
        kn[i, 0:4, :] = qkv[0, :, pl.ds((8 + i) * HD, HD)].astype(F32)
        kn[2 + i, 0:4, :] = qkv[0, :, pl.ds((10 + i) * HD, HD)].astype(F32)
    length = bc.shape[0]
    scaling = HD ** (-0.5)
    seen = iota((16, length), 1) < byte_len[0, 0]
    causal = iota((16, 16), 1) <= iota((16, 16), 0) % 4
    for i in range(2):
        q_i = qs[pl.ds(i * 16, 16), :].astype(BF16)
        old = dot_t(q_i, bc[:, pl.ds(i * HD, HD)]) * scaling
        old = jnp.where(seen, old, NEG_FILL)
        new = dot_t(q_i, kn[i].astype(BF16)) * scaling
        new = jnp.where(causal, new, NEG_FILL)
        top = jnp.maximum(jnp.max(old, axis=1, keepdims=True), jnp.max(new, axis=1, keepdims=True))
        old, new = jnp.exp(old - top), jnp.exp(new - top)
        total = jnp.sum(old, axis=1, keepdims=True) + jnp.sum(new, axis=1, keepdims=True)
        old, new = (old / total).astype(BF16), (new / total).astype(BF16)
        os[pl.ds(i * 16, 16), :] = dot(old, bc[:, pl.ds((2 + i) * HD, HD)]) + dot(
            new, kn[2 + i].astype(BF16))
        for hh in range(4):
            xm[pl.ds((2 * i + hh // 2) * 4, 4), pl.ds((hh % 2) * HD, HD)] = (
                hidden[0, :, pl.ds((i * 4 + hh) * HD, HD)].astype(F32) + os[pl.ds(i * 16 + hh * 4, 4), :]
            )
    rows_16 = xm[...].astype(BF16)
    XS[me_p] = jnp.concatenate([rows_16, marks.astype(BF16)], axis=1)
    rows_s = over_streams(XS, xs_sems).start()

    ups.forward()
    rows_s.forward()

    tiles = kv_x.total(KP[x]).astype(BF16)
    tall = rows_own // 16
    for b in range(2 * tall):
        KS[b // (2 * tall // Z), b % (2 * tall // Z)] = tiles[
            (b // 2) * 16:(b // 2 + 1) * 16, (b % 2) * HD:(b % 2 + 1) * HD]
    kv_z = Axis(KS, KZ, z, Z, z_peer, kz_s, kz_r).start()

    o_col = jnp.sum(
        jnp.where(iota((S, T), 1) == me_t, owners[...].astype(F32), 0.0), axis=1, keepdims=True)
    eye = iota((S, S), 0) == iota((S, S), 1)
    o_row = jnp.sum(jnp.where(eye, o_col, 0.0), axis=0, keepdims=True)
    same = o_col == o_row
    rank_col = jnp.sum(
        jnp.where(same & (iota((S, S), 1) < iota((S, S), 0)), 1.0, 0.0), axis=1, keepdims=True)
    own_col = iota((S, 1), 0) == me_s
    my_owner = jnp.sum(jnp.where(own_col, o_col, 0.0), axis=0, keepdims=True)
    my_rank = jnp.sum(jnp.where(own_col, rank_col, 0.0), axis=0, keepdims=True)
    tgt_col = jnp.where(o_col == me_s.astype(F32), rank_col, -1.0)
    W = S * 16
    stream_of = lambda lane: (lane // 16 % Y) * 2 + lane // (16 * Y)
    tgt = jnp.sum(
        jnp.where(stream_of(iota((S, W), 1)) == iota((S, W), 0), tgt_col, 0.0), axis=0, keepdims=True)

    rows_s.recv()
    r, l = iota((16, W), 0), iota((16, W), 1)
    every = XS[...].reshape(W, 256 + HD)
    picked = (tgt == ((r % 8) // 4).astype(F32)) & (l % 4 == r % 4)
    halves = []
    for part in range(2):
        pick = jnp.where(picked & ((l % 16) // 4 == (r // 8) * 2 + part), 1.0, 0.0).astype(BF16)
        halves.append(dot(pick, every[:, :256]).astype(BF16))
    XT[me_t] = jnp.concatenate(halves, axis=1)
    rows_t = over_tp(XT, xt_sems, True).start()
    slot_marks = []
    for j in range(2):
        pick = jnp.where((tgt == float(j)) & (l % 16 == 0), 1.0, 0.0).astype(BF16)
        slot_marks.append(dot(pick, every[:, 256:]))
    slot_marks = jnp.where((lanes % 8) // 4 == 0, slot_marks[0], slot_marks[1])[0:8, :]

    locals_[3].wait()

    def query_part(source, total):
        base = pl.multiple_of(source * (Z * 256), Z * 256)
        for zb in range(Z):
            total = total + dot(UT[source * Z + zb], wq[pl.ds(base + zb * 256, 256), :])
        return total

    folded = query_part(x, jnp.zeros((rows_own, HD), F32))
    KA[z] = kv_z.total(KS[z]).astype(BF16)
    kv_all = Axis(KA, KA, z, Z, z_peer, ka_s, ka_r).start()
    rows_t.forward()
    for d in range(1, X):
        ups.arrived(d)
        folded = query_part(lax.rem(x + X - d, X), folded)
        if d == 1:
            kv_all.recv()
            for b in range(2 * tall):
                MK[me_p, pl.ds((b // 2) * 16, 16), pl.ds((b % 2) * HD, HD)] = KA[
                    b // (2 * tall // Z), b % (2 * tall // Z)]
            keyvals_s = over_streams(MK, mk_sems).start()
    MQ[me_p] = folded.astype(BF16)
    queries_s = over_streams(MQ, mq_sems).start()

    locals_[0].wait()
    rows_t.recv()
    rows_all = XT[...].reshape(T * 16, 512)
    N = T * 8

    def project(top, bottom, width):
        upper = dot(rows_all, top).reshape(T, 16, width)[:, :8]
        lower = dot(rows_all, bottom).reshape(T, 16, width)[:, 8:]
        return (upper + lower).reshape(N, width)

    expanded = project(up[0:512, :], up[512:1024, :], up.shape[1]).astype(BF16).astype(F32)
    squared = expanded * expanded
    high = squared.astype(BF16)
    low = (squared - high.astype(F32)).astype(BF16)
    ones = jnp.ones((8, up.shape[1]), BF16)
    spot = slot_marks[:, :N] if N <= HD else jnp.concatenate([slot_marks] * (N // HD), axis=1)
    spot = jnp.where(iota((8, N), 1) // 8 == me_t, spot, 0.0)
    SQZ[z] = jnp.where(iota((8, N), 0) == 0, dot_t(ones, high) + dot_t(ones, low), spot)
    squares_z = Axis(SQZ, SQZ, z, Z, z_peer, sqz_s, sqz_r).start()
    keyvals_s.forward()
    queries_s.forward()
    SQX[x] = squares_z.total(SQZ[z])
    squares_x = Axis(SQX, SQX, x, X, x_peer, sqx_s, sqx_r).start()

    keyvals_s.recv()
    weights = MK[...].reshape(S * rows_own, 2 * HD)
    keyvals = project(weights[:512], weights[512:], 2 * HD)
    keys = keyvals[:, :HD].astype(BF16)
    queries_s.recv()
    weights = MQ[...].reshape(S * rows_own, HD)
    raw[...] = project(weights[:512], weights[512:], HD)

    locals_[4].wait()
    locals_[6].wait()
    locals_[5].wait()
    slots, span = ck.shape[0], ck.shape[1]
    len_col = jnp.sum(
        jnp.where(iota((N, slots), 0) // 4 == iota((N, slots), 1), coarse_len[...].astype(F32), 0.0),
        axis=1, keepdims=True)
    summed = squares_x.total(SQX[x])
    inverse_row = lax.rsqrt(summed[0:1, :] / (up.shape[1] * T) + EPSILON)
    marked = summed[1:2, :] > 0.5
    inverse = jnp.sum(
        jnp.where(iota((N, N), 0) == iota((N, N), 1), inverse_row, 0.0), axis=1, keepdims=True)
    cols[...] = jnp.where(iota((N, HD), 1) == 0, inverse, len_col)
    values = (keyvals[:, HD:] * inverse).astype(BF16)

    block, per = Z * 8, min(8, Z * 2)
    chunks = Z * 2 // per
    by_chunk = lambda col: col.reshape(chunks, per * 4, 1)
    row_old, lane_old = iota((per * 4, per * span), 0), iota((per * 4, per * span), 1)
    position = jnp.where(lane_old // span == row_old // 4, lane_old % span, span).astype(F32)
    lane_new, row_new = iota((block, N), 1), iota((block, N), 0)
    back_x = Axis(PX, RX, x, X, x_peer, px_s, px_r)
    for d in far_first(X) + [0]:
        to = lax.rem(x + d, X)
        at_row = pl.ds(pl.multiple_of(to * block, block), block)
        at_slot = pl.ds(to * (Z * 2), Z * 2)
        queries = raw[at_row, :].astype(BF16)
        factor, filled = cols[at_row, 0:1] * scaling, cols[at_row, 1:2]
        old = bdot_t(queries.reshape(chunks, per * 4, HD), ck[at_slot].reshape(chunks, per * span, HD))
        new = dot_t(queries, keys)
        row = row_new + to * block
        allowed = (lane_new // 4 == row // 4) & (lane_new % 4 <= row % 4) & marked
        old = jnp.where(position[None] < by_chunk(filled), old * by_chunk(factor), NEG_FILL)
        new = jnp.where(allowed, new * factor * inverse_row, NEG_FILL)
        top = jnp.maximum(
            jnp.max(old, axis=2, keepdims=True).reshape(block, 1), jnp.max(new, axis=1, keepdims=True))
        old, new = jnp.exp(old - by_chunk(top)), jnp.exp(new - top)
        total = jnp.sum(old, axis=2, keepdims=True).reshape(block, 1) + jnp.sum(
            new, axis=1, keepdims=True)
        old, new = (old / by_chunk(total)).astype(BF16), (new / total).astype(BF16)
        attended = bdot(old, cv[at_slot].reshape(chunks, per * span, HD)).reshape(block, HD)
        attended = (attended + dot(new, values)).astype(BF16)
        PX[to] = dot(attended, wr[...]).astype(BF16)
        if d:
            back_x.copy(d, PX.at[to], RX.at[x]).start()

    for comm in comms:
        if comm is not back_x:
            comm.finish()

    summed = back_x.total(PX[x]).reshape(Z, 8, 1024)
    PZ[...] = jnp.concatenate([summed[:, :, :512], summed[:, :, 512:]], axis=1).astype(BF16)
    back_z = Axis(PZ, RZ, z, Z, z_peer, pz_s, pz_r).start()
    RB[me_p] = back_z.total(PZ[z]).astype(BF16)
    back_s = over_streams(RB, rb_sems).start()
    back_s.recv()

    home = (stream_of(l).astype(F32) == my_owner) & (((l % 8) // 4).astype(F32) == my_rank)
    home = home & (l % 4 == last_col) & ((l % 16) // 8 == r // 8)
    back = RB[...].reshape(W, 512)
    latest = jnp.zeros((16, 256), F32)
    for part in range(2):
        pick = jnp.where(home & ((r // 4) % 2 == part), 1.0, 0.0).astype(BF16)
        latest = latest + dot(pick, back[:, part * 256:(part + 1) * 256])
    earlier = jnp.zeros((16, 256), F32)
    for k in range(4):
        earlier = jnp.where(
            iota((16, 256), 0) // 4 == k, prev[0:1, pl.ds(k * 256, 256)].astype(F32), earlier)
    latest = jnp.where(last_col < 0, earlier, latest)
    xm[...] = rows_16.astype(F32) + latest
    for k in range(4):
        out_ref[0, :, pl.ds(k * 256, 256)] = xm[pl.ds(k * 4, 4), :].astype(BF16)

    for comm in (back_x, back_z, back_s):
        comm.finish()


def shards(
    S, X, Z,
    hidden_in, byte_qkv, byte_cache, byte_len, flags, coarse_prev, owner_map, up_weight,
    coarse_gain, query_weight, keyval_weight, return_weight, coarse_cache, coarse_len,
):
    T = X * Z
    part = up_weight.shape[1]
    gains = coarse_gain.reshape(T, part // HD, HD)
    owners = owner_map.transpose(1, 2, 0)
    rows = up_weight.shape[0] // S
    heads2 = 2 * HD
    vm = pl.BlockSpec(memory_space=pltpu.VMEM)
    dma = pltpu.SemaphoreType.DMA
    pair = lambda *shape: [dma(shape), dma(shape)]
    scratch = [
        pltpu.SMEM((1, 1), I32),
        pltpu.SMEM(flags.shape, I32),
        pltpu.VMEM(hidden_in.shape, BF16),
        pltpu.VMEM(byte_qkv.shape, BF16),
        pltpu.VMEM(coarse_prev.shape, BF16),
        pltpu.VMEM((S, T), I32),
        pltpu.VMEM(gains.shape[1:], F32),
        pltpu.VMEM(coarse_len.shape, I32),
        pltpu.VMEM((rows, part), BF16),
        pltpu.VMEM(byte_cache.shape[1:], BF16),
        pltpu.VMEM(up_weight.shape, BF16),
        pltpu.VMEM(query_weight.shape, BF16),
        pltpu.VMEM(keyval_weight.shape, BF16),
        pltpu.VMEM(return_weight.shape, BF16),
        pltpu.VMEM((coarse_cache.shape[1], coarse_cache.shape[3], HD), BF16),
        pltpu.VMEM((coarse_cache.shape[1], coarse_cache.shape[3], HD), BF16),
        pltpu.VMEM((32, HD), F32),
        pltpu.VMEM((4, 16, HD), F32),
        pltpu.VMEM((32, HD), F32),
        pltpu.VMEM((16, 256), F32),
        pltpu.VMEM((T * 8, HD), F32),
        pltpu.VMEM((T * 8, HD), F32),
        pltpu.VMEM((S, 16, 256 + HD), BF16),
        pltpu.VMEM((T, 16, 512), BF16),
        pltpu.VMEM((T, rows, part), BF16),
        pltpu.VMEM((S, rows, HD), BF16),
        pltpu.VMEM((S, rows, heads2), BF16),
        pltpu.VMEM((X, rows, heads2), BF16),
        pltpu.VMEM((X, rows, heads2), BF16),
        pltpu.VMEM((Z, rows // (8 * Z), 16, HD), BF16),
        pltpu.VMEM((Z, rows // (8 * Z), 16, HD), BF16),
        pltpu.VMEM((Z, rows // (8 * Z), 16, HD), BF16),
        pltpu.VMEM((Z, 8, T * 8), F32),
        pltpu.VMEM((X, 8, T * 8), F32),
        pltpu.VMEM((X, Z * 8, 1024), BF16),
        pltpu.VMEM((X, Z * 8, 1024), BF16),
        pltpu.VMEM((Z, 16, 512), BF16),
        pltpu.VMEM((Z, 16, 512), BF16),
        pltpu.VMEM((S, 16, 512), BF16),
        dma((16,)),
    ]
    Y = S // 2
    on_streams = [dma((Y,)), dma((Y,)), dma((2, 1)), dma((2, 1))]
    on_tp = [dma((Z,)), dma((Z,)), dma((X, Z)), dma((X, Z))]
    scratch += [on_streams, on_tp, on_tp] + [on_streams] * 3
    for shape in ((X,), (Z,), (Z,), (Z,), (X,), (X,), (Z,)):
        scratch += pair(*shape)
    return pl.pallas_call(
        functools.partial(kernel, S, X, Z),
        out_shape=jax.ShapeDtypeStruct(hidden_in.shape, BF16),
        in_specs=[pl.BlockSpec(memory_space=pltpu.HBM)] * 14,
        out_specs=vm,
        scratch_shapes=scratch,
        compiler_params=pltpu.CompilerParams(
            collective_id=0, has_side_effects=True, vmem_limit_bytes=60 * 1024 * 1024
        ),
        name="decode",
    )(
        byte_len.reshape(1, 1), flags, hidden_in, byte_qkv, coarse_prev, owners, gains, coarse_len,
        byte_cache, up_weight, query_weight, keyval_weight, return_weight, coarse_cache,
    )


def solution(mesh):
    S, T = mesh.shape["streams"], mesh.shape["tp"]
    X = 4 if T >= 16 else 2
    return jax.shard_map(
        functools.partial(shards, S, X, T // X),
        mesh=mesh,
        in_specs=(
            P(("streams", "tp"), None, None),
            P(("streams", "tp"), None, None),
            P(("streams", "tp"), None, None),
            P(("streams", "tp")),
            P(("streams", "tp"), None),
            P(("streams", "tp"), None),
            P(),
            P(None, "tp"),
            P(),
            P(None, "tp"),
            P("tp", None),
            P("tp", None),
            P("streams", None, "tp", None, None),
            P("streams", None),
        ),
        out_specs=P(("streams", "tp"), None, None),
        check_vma=False,
    )
```
